256 devices in a mesh: seq: 8 (over z), head: 8 (over x, core), rep: 4 (over y).
Axes of the slice: x: 4, y: 4, z: 8, core: 2. Of those that a mesh axis runs over, the one named last changes fastest.
Arguments:
- queries: bfloat16 [16384, 8192], P(('rep', 'seq', 'head')), parts along dimension 0, may hold values from -6 to 6
- keys: bfloat16 [16384, 1024], P(('rep', 'seq', 'head')), parts along dimension 0, may hold values from -4.6 to 4.6
- values: bfloat16 [16384, 1024], P(('rep', 'seq', 'head')), parts along dimension 0, may hold values from -6 to 6
- counts: int32 [256, 8], P(('rep', 'seq', 'head')), parts along dimension 0, may hold values from 0 to 32, as said below
- offsets: int32 [256, 8], P(('rep', 'seq', 'head')), parts along dimension 0, may hold values from 0 to 64, as said below
- tree_ids: int32 [256, 8], P(('rep', 'seq', 'head')), parts along dimension 0, may hold values from 0 to 3
- block_lists: int32 [32, 16, 7], P(('rep', 'seq')), parts along dimension 0, may hold values from -1 to 14, as said below
Outputs:
- attended: bfloat16 [16384, 8192], P(('rep', 'seq', 'head')), parts along dimension 0
The draws below stay inside these ranges and needn't reach their ends.
There are 4 independent parts, one for each index of `rep`. The reference program is written for one: setup_inputs(seed, part) draws one part's arguments, and reference() takes and returns one part's arrays. A program takes and returns all parts, laid end to end along the dimension named above; each array names one. Nothing has to cross between parts.
Inputs may be any that keep to these rules, and one draw needn't show every extreme that they name: Each worker's counts sum to 64 and are at most 32; in every draw one shard receives exactly 32 rows from every worker. For each worker the segments [offsets, offsets + counts) over all shards tile its rows 0 to 63. Entry k of block_lists[s, b] is the (k + 1)-th nearest ancestor of block b in a tree over the blocks of shard s, each ancestor an earlier block; -1 past the root.
All inputs are finite; a program needn't handle non-finite values.
Results may differ from the reference program's by a relative error of at most 0.0024.
Values may be sent and summed in bfloat16 or wider, within the bound.
A program may use at most 64 MiB of HBM per device.

```python
import math
import jax
import jax.numpy as jnp
from jax import lax

QUERY_HEADS = 64
KEY_VALUE_HEADS = 8
HEAD_SIZE = 128
TOK_W = 64
MASK_BLOCK_ROWS = 128
ANCESTOR_COUNT = 7
TREES = 4
SLOT = 32
WORKERS = 64
SLAB_TOKENS = 4096
QB = 16
N_SEQ = 8


def route_tables(key):
    key = jax.random.fold_in(key, 7)
    key_hot, key_perm, key_move = jax.random.split(key, 3)
    hottest = jax.random.randint(key_hot, (), 0, N_SEQ)
    remain_count = N_SEQ - 1
    spread_rows = TOK_W - SLOT
    evenly = spread_rows // remain_count
    leftover = spread_rows % remain_count
    column_ids = jnp.arange(remain_count, dtype=jnp.int32)
    remain = jnp.full((WORKERS, remain_count), evenly, jnp.int32) + (column_ids < leftover).astype(jnp.int32)[None, :]
    for attempt in range(12):
        key_a, key_b, key_c = jax.random.split(jax.random.fold_in(key_move, attempt), 3)
        source = jax.random.randint(key_a, (WORKERS, 1), 0, remain_count)
        target = jax.random.randint(key_b, (WORKERS, 1), 0, remain_count)
        amount = jax.random.randint(key_c, (WORKERS, 1), 0, SLOT + 1)
        one_source = (column_ids[None, :] == source).astype(jnp.int32)
        one_target = (column_ids[None, :] == target).astype(jnp.int32)
        holding = jnp.sum(remain * one_source, axis=1, keepdims=True)
        space_left = SLOT - jnp.sum(remain * one_target, axis=1, keepdims=True)
        amount = jnp.minimum(amount, jnp.minimum(holding, space_left))
        amount = jnp.where(source == target, 0, amount)
        remain = remain - amount * one_source + amount * one_target
    shards = jnp.arange(N_SEQ, dtype=jnp.int32)
    chosen = jnp.clip(shards - (shards > hottest).astype(jnp.int32), 0, remain_count - 1)
    counts = jnp.where(shards[None, :] == hottest, SLOT, remain[:, chosen])
    scores = jax.random.randint(key_perm, (WORKERS, N_SEQ), 0, 1 << 20) * N_SEQ + shards[None, :]
    ordering = jnp.argsort(scores, axis=1)
    in_order = jnp.take_along_axis(counts, ordering, axis=1)
    starts = jnp.cumsum(in_order, axis=1) - in_order
    inverse = jnp.argsort(ordering, axis=1)
    offsets = jnp.take_along_axis(starts, inverse, axis=1)
    return (counts.astype(jnp.int32), offsets.astype(jnp.int32))


def draw_counts(key, part):
    tables = route_tables(key)
    return tables[0]


def draw_offsets(key, part):
    tables = route_tables(key)
    return tables[1]


def draw_block_lists(key, part):
    key = jax.random.fold_in(key, 13)
    blocks = jnp.arange(QB, dtype=jnp.int32)
    shard_ids = jnp.arange(N_SEQ, dtype=jnp.int32)
    jump_back = jax.random.randint(key, (N_SEQ, QB), 0, 4)
    forced = (shard_ids[:, None] == 0) & (blocks[None, :] == QB - 1)
    jump_back = jnp.where(forced, 0, jump_back)
    parents = jnp.where(blocks[None, :] == 0, -1, jnp.maximum(blocks[None, :] - 1 - jump_back, 0))
    current = parents
    ancestry = []
    for depth_step in range(ANCESTOR_COUNT):
        ancestry.append(current)
        following = jnp.take_along_axis(parents, jnp.maximum(current, 0), axis=1)
        current = jnp.where(current >= 0, following, -1)
    return jnp.stack(ancestry, axis=2).astype(jnp.int32)


def draw_queries(key, part):
    key = jax.random.fold_in(key, 31)
    return jnp.clip(1.6 * jax.random.normal(key, (SLAB_TOKENS, QUERY_HEADS * HEAD_SIZE), jnp.float32), -6.0, 6.0).astype(jnp.bfloat16)


def draw_keys(key, part):
    key = jax.random.fold_in(key, 21)
    return jnp.clip(1.25 * jax.random.normal(key, (SLAB_TOKENS, KEY_VALUE_HEADS * HEAD_SIZE), jnp.float32), -4.6, 4.6).astype(jnp.bfloat16)


def place_ends(values, key, smallest, largest):
    spot = [jax.random.randint(jax.random.fold_in(key, axis), (), 0, length) for axis, length in enumerate(values.shape)]
    widest = values.shape.index(max(values.shape))
    next_to = spot[:widest] + [(spot[widest] + 1) % values.shape[widest]] + spot[widest + 1:]
    return values.at[tuple(spot)].set(smallest).at[tuple(next_to)].set(largest)


def levels(key, extent, cuts, low, high):
    loudness, own = 1.0, jax.random.fold_in(key, 6)
    for position, shards_of in cuts:
        heights = jnp.exp(jax.random.uniform(jax.random.fold_in(own, position), (shards_of,), jnp.float32, low / len(cuts), high / len(cuts)))
        loudness = loudness * jnp.repeat(heights, extent[position] // shards_of).reshape([-1 if axis == position else 1 for axis in range(len(extent))])
    return loudness


def gaussian(own_key, extent, deviation, bound, cuts=(), held_as=jnp.bfloat16):
    drawn = deviation * jax.random.normal(own_key, extent, jnp.float32)
    if cuts:
        drawn = drawn * levels(own_key, extent, cuts, -0.22, 0.18)
    return jnp.clip(drawn, -bound, bound).astype(held_as)


def setup_inputs(seed: int = 0, part: int = 0) -> dict:
    key_of = jax.random.split(jax.random.key(seed), 8)
    own_keys = jax.random.split(jax.random.fold_in(key_of[7], part), 8)
    queries = draw_queries(jax.random.fold_in(jax.random.fold_in(key_of[7], part), 71), part)
    keys = draw_keys(jax.random.fold_in(jax.random.fold_in(key_of[7], part), 71), part)
    values = gaussian(own_keys[2], (SLAB_TOKENS, KEY_VALUE_HEADS * HEAD_SIZE), 1.0, 6.0, ((0, 64),))
    counts = draw_counts(jax.random.fold_in(jax.random.fold_in(key_of[7], part), 71), part)
    offsets = draw_offsets(jax.random.fold_in(jax.random.fold_in(key_of[7], part), 71), part)
    tree_ids = place_ends(jax.random.randint(own_keys[5], (WORKERS, N_SEQ), 0, TREES), jax.random.fold_in(own_keys[5], 1), 0, TREES - 1).astype(jnp.int32)
    block_lists = draw_block_lists(jax.random.fold_in(jax.random.fold_in(key_of[7], part), 71), part)
    return dict(queries=queries, keys=keys, values=values, counts=counts, offsets=offsets, tree_ids=tree_ids, block_lists=block_lists)


def reference(queries, keys, values, counts, offsets, tree_ids, block_lists):
    query_group_width = QUERY_HEADS // KEY_VALUE_HEADS
    score_scale = 1.0 / math.sqrt(HEAD_SIZE)
    row_count = WORKERS * SLOT
    slot_pos = jnp.arange(SLOT, dtype=jnp.int32)
    worker_ids = jnp.arange(WORKERS, dtype=jnp.int32)
    block_pos = jnp.arange(MASK_BLOCK_ROWS, dtype=jnp.int32)

    def one_shard(shard_idx):
        starts = offsets[:, shard_idx]
        amounts = counts[:, shard_idx]
        tree_of = tree_ids[:, shard_idx]
        slot_live = slot_pos[None, :] < amounts[:, None]
        source = worker_ids[:, None] * TOK_W + starts[:, None] + jnp.where(slot_live, slot_pos[None, :], 0)
        source = source.reshape(-1).astype(jnp.int32)
        row_live = slot_live.reshape(-1)
        row_tree = jnp.repeat(tree_of, SLOT)
        query_row_slice = queries[source]
        key_row_slice = keys[source]
        value_row_slice = values[source]
        ancestry = block_lists[shard_idx]

        def one_block(block_idx):
            key_blocks = jnp.concatenate([ancestry[block_idx], block_idx[None]]).astype(jnp.int32)
            valid_block = key_blocks >= 0
            key_row_values = (jnp.maximum(key_blocks, 0)[:, None] * MASK_BLOCK_ROWS + block_pos[None, :]).reshape(-1)
            query_row_values = block_idx * MASK_BLOCK_ROWS + block_pos
            key_ok = jnp.repeat(valid_block, MASK_BLOCK_ROWS) & row_live[key_row_values]
            same_tree = row_tree[query_row_values][:, None] == row_tree[key_row_values][None, :]
            diagonal = jnp.repeat(jnp.arange(ANCESTOR_COUNT + 1) == ANCESTOR_COUNT, MASK_BLOCK_ROWS)
            causal = jnp.logical_not(diagonal)[None, :] | (jnp.tile(block_pos, ANCESTOR_COUNT + 1)[None, :] <= block_pos[:, None])
            allowed = key_ok[None, :] & same_tree & causal
            query_block_tile = query_row_slice[query_row_values].astype(jnp.float32).reshape(MASK_BLOCK_ROWS, KEY_VALUE_HEADS, query_group_width, HEAD_SIZE)
            key_block_tile = key_row_slice[key_row_values].astype(jnp.float32).reshape((ANCESTOR_COUNT + 1) * MASK_BLOCK_ROWS, KEY_VALUE_HEADS, HEAD_SIZE)
            value_block_tile = value_row_slice[key_row_values].astype(jnp.float32).reshape((ANCESTOR_COUNT + 1) * MASK_BLOCK_ROWS, KEY_VALUE_HEADS, HEAD_SIZE)
            scores = jnp.einsum('qhgd,khd->hgqk', query_block_tile, key_block_tile) * score_scale
            scores = jnp.where(allowed[None, None], scores, jnp.float32(-1e+30))
            row_max = lax.optimization_barrier(jnp.max(scores, axis=-1, keepdims=True))
            weights = jnp.exp(scores - row_max)
            totals = lax.optimization_barrier(jnp.sum(weights, axis=-1))
            rounded = lax.optimization_barrier(weights.astype(jnp.bfloat16)).astype(jnp.float32)
            blended = jnp.einsum('hgqk,khd->qhgd', rounded, value_block_tile) / jnp.transpose(totals, (2, 0, 1))[..., None]
            return blended.reshape(MASK_BLOCK_ROWS, QUERY_HEADS * HEAD_SIZE).astype(jnp.bfloat16)
        shard_out = lax.map(one_block, jnp.arange(QB, dtype=jnp.int32))
        return shard_out.reshape(row_count, QUERY_HEADS * HEAD_SIZE)
    all_out = lax.map(one_shard, jnp.arange(N_SEQ, dtype=jnp.int32))
    positions = jnp.arange(TOK_W, dtype=jnp.int32)
    member = ((offsets[:, None, :] <= positions[None, :, None]) & (positions[None, :, None] < offsets[:, None, :] + counts[:, None, :])).astype(jnp.int32)
    segment = lax.optimization_barrier(jnp.sum(member * jnp.arange(N_SEQ, dtype=jnp.int32)[None, None, :], axis=-1))
    begin_at = lax.optimization_barrier(jnp.sum(member * offsets[:, None, :], axis=-1))
    flat_index = segment * row_count + worker_ids[:, None] * SLOT + positions[None, :] - begin_at
    flat_index = flat_index.reshape(-1).astype(jnp.int32)
    return all_out.reshape(N_SEQ * row_count, QUERY_HEADS * HEAD_SIZE)[flat_index]
```

```python
import math

import jax
import jax.numpy as jnp
from jax import lax
from jax.experimental import pallas as pl
from jax.experimental.pallas import tpu as pltpu
from jax.sharding import PartitionSpec as P

MESH = pl.DeviceIdType.MESH
KEY_VALUE_HEADS = 8
GROUP = 8
HEAD_SIZE = 128
TOK_W = 64
ANCESTOR_COUNT = 7
QB = 16
N_SEQ = 8
N_HEAD = 8
ROW = N_HEAD * TOK_W
WIDE = GROUP * HEAD_SIZE
QROWS = GROUP * TOK_W
NEG = -1e30
FACTOR = math.log2(math.e) / math.sqrt(HEAD_SIZE)
NT = (((1,), (1,)), ((), ()))


def kernel(
    cnt_ref, off_ref, tree_ref, bl_ref, q_ref, k_ref, v_ref, out_ref,
    qbuf, kv, feat, ids, anc, qa, sbuf, mx, den, acc, stage,
    own_sem, kv_s, kv_r, id_s, id_r, q_s, q_r, ring_s, ring_r, idr_s, idr_r, an_s, an_r, o_s, o_r,
):
    z = lax.axis_index("seq")
    h = lax.axis_index("head")
    up = lax.rem(z + 1, N_SEQ)
    down = lax.rem(z + N_SEQ - 1, N_SEQ)

    barrier = pltpu.get_barrier_semaphore()
    for d in range(1, N_HEAD):
        pl.semaphore_signal(barrier, inc=1, device_id={"head": lax.rem(h + d, N_HEAD)}, device_id_type=MESH)
    pl.semaphore_signal(barrier, inc=1, device_id={"seq": up}, device_id_type=MESH)
    pl.semaphore_signal(barrier, inc=1, device_id={"seq": down}, device_id_type=MESH)

    lane1 = lax.broadcasted_iota(jnp.int32, (1, 128), 1)
    cls = jnp.zeros((1, 128), jnp.float32)
    for s in range(N_SEQ):
        start = off_ref[0, s]
        member = (lane1 >= start) & (lane1 < start + cnt_ref[0, s])
        cls = jnp.where(member, (s * 4 + tree_ref[0, s]).astype(jnp.float32), cls)
    ids[z, h] = cls
    lane_block = (lane1 - 32) >> 2
    for b in range(QB):
        hit = jnp.zeros((1, 128), jnp.float32)
        for k in range(ANCESTOR_COUNT):
            e = bl_ref[0, b, k]
            hit = jnp.where((lane_block == e) & (lane1 >= 32), 1.0, hit)
        anc[z, b] = hit

    def cols(p):
        return pl.ds(pl.multiple_of(p * HEAD_SIZE, HEAD_SIZE), HEAD_SIZE)

    def wide(p):
        return pl.ds(pl.multiple_of(p * WIDE, WIDE), WIDE)

    mine = pl.ds(pl.multiple_of(z * ROW + h * TOK_W, TOK_W), TOK_W)
    left, right = pl.ds(0, HEAD_SIZE), pl.ds(HEAD_SIZE, HEAD_SIZE)
    own = [
        pltpu.make_async_copy(k_ref.at[:, cols(h)], kv.at[mine, left], own_sem.at[0]),
        pltpu.make_async_copy(v_ref.at[:, cols(h)], kv.at[mine, right], own_sem.at[1]),
        pltpu.make_async_copy(q_ref.at[:, wide(h)], qbuf.at[h], own_sem.at[2]),
    ]
    for c in own:
        c.start()

    pl.semaphore_wait(barrier, N_HEAD + 1)

    def remote(src, dst, s_sem, r_sem, **where):
        return pltpu.make_async_remote_copy(
            src_ref=src, dst_ref=dst, send_sem=s_sem, recv_sem=r_sem, device_id=where, device_id_type=MESH
        )

    first = []
    for d in range(1, N_HEAD):
        p = lax.rem(h + d, N_HEAD)
        first.append(remote(k_ref.at[:, cols(p)], kv.at[mine, left], kv_s.at[d, 0], kv_r.at[d, 0], head=p))
        first.append(remote(v_ref.at[:, cols(p)], kv.at[mine, right], kv_s.at[d, 1], kv_r.at[d, 1], head=p))
        first.append(remote(ids.at[z, h], ids.at[z, h], id_s.at[d], id_r.at[d], head=p))
    for c in first:
        c.start()
    own[0].wait()
    own[1].wait()
    for c in first:
        c.wait_recv()

    half = ROW // 2

    def rows(r, j):
        return pl.ds(pl.multiple_of(r * ROW + j * half, half), half)

    def step(way, t):
        src = lax.rem(z + N_SEQ - t, N_SEQ) if way == 0 else lax.rem(z + t, N_SEQ)
        to = up if way == 0 else down
        halves = (0, 1) if t < 3 else (way,)
        out = [
            remote(kv.at[rows(src, j)], kv.at[rows(src, j)], ring_s.at[way, t, j], ring_r.at[way, t, j], seq=to)
            for j in halves
        ]
        if t < 3 or way == 0:
            out.append(remote(ids.at[src], ids.at[src], idr_s.at[way, t], idr_r.at[way, t], seq=to))
            out.append(remote(anc.at[src], anc.at[src], an_s.at[way, t], an_r.at[way, t], seq=to))
        return out

    steps = [[step(way, t) for t in range(4)] for way in range(2)]
    for way in range(2):
        for c in steps[way][0]:
            c.start()
    queries = [
        remote(
            q_ref.at[:, wide(lax.rem(h + d, N_HEAD))], qbuf.at[h], q_s.at[d], q_r.at[d], head=lax.rem(h + d, N_HEAD)
        )
        for d in range(1, N_HEAD)
    ]
    for c in queries:
        c.start()
    for t in range(1, 5):
        for i in range(4):
            for way in range(2):
                if i < len(steps[way][t - 1]):
                    steps[way][t - 1][i].wait_recv()
                    if t < 4:
                        if t < 3:
                            steps[way][t][i].start()
                        elif way == 0 and i != 1:
                            steps[way][t][(0, 0, 1, 2)[i]].start()
                        elif way == 1 and i == 1:
                            steps[way][t][0].start()
    own[2].wait()
    for c in queries:
        c.wait_recv()

    lane = lax.broadcasted_iota(jnp.int32, (TOK_W, 128), 1)
    tok = lax.broadcasted_iota(jnp.int32, (TOK_W, 128), 0)

    def column(row):
        return jnp.sum(jnp.where(lane == tok, row, 0.0), axis=1, keepdims=True)

    def key_features(w, carry):
        c = column(ids[w // N_HEAD, lax.rem(w, N_HEAD)])
        hot = (lane.astype(jnp.float32) == c) | (lane == 32 + w)
        feat[pl.ds(pl.multiple_of(w * TOK_W, TOK_W), TOK_W), :] = jnp.where(hot, 1.0, 0.0).astype(jnp.bfloat16)
        return carry

    lax.fori_loop(0, (z + 1) * N_HEAD, key_features, 0)

    row_id = lax.broadcasted_iota(jnp.int32, (QROWS, ROW), 0)
    col_id = lax.broadcasted_iota(jnp.int32, (QROWS, ROW), 1)

    def tile(d, carry):
        p = lax.rem(h + d, N_HEAD)
        w = z * N_HEAD + p
        b = w // 4
        c = column(ids[z, p])
        shard = jnp.floor(c * 0.25)
        looks = jnp.zeros((TOK_W, 128), jnp.float32)
        for s in range(N_SEQ):
            looks = jnp.where(shard == float(s), anc[s, b], looks)
        worker = lane - 32
        own_block = ((worker >> 2) == b) & (worker <= w)
        fine = jnp.where(
            lane < 32,
            jnp.where(lane.astype(jnp.float32) == c, 1.0, 0.0),
            jnp.where((lane >= 96) | own_block, 1.0, looks),
        )
        penalty = jnp.where(fine > 0.5, 0.0, NEG).astype(jnp.bfloat16)
        for g in range(GROUP):
            r = pl.ds(g * TOK_W, TOK_W)
            qa[r, 0:HEAD_SIZE] = qbuf[p, :, g * HEAD_SIZE : (g + 1) * HEAD_SIZE]
            qa[r, HEAD_SIZE:] = penalty

        def chunk_rows(i):
            return pl.ds(pl.multiple_of(i * ROW, ROW), ROW)

        def scores(i):
            keys = jnp.concatenate([kv[chunk_rows(i), 0:HEAD_SIZE], feat[chunk_rows(i), :]], axis=1)
            return lax.dot_general(qa[...], keys, NT, preferred_element_type=jnp.float32)

        def fold(x, op):
            return op(op(x[:, 0:128], x[:, 128:256]), op(x[:, 256:384], x[:, 384:512]))

        s = scores(z)
        late = ((col_id >> 6) == p) & ((col_id & 63) > (row_id & 63))
        s = jnp.where(late, NEG, s)
        sbuf[z] = s
        mx[...] = fold(s, jnp.maximum)

        def find(i, carry):
            s = scores(i)
            sbuf[i] = s
            mx[...] = jnp.maximum(mx[...], fold(s, jnp.maximum))
            return carry

        lax.fori_loop(0, z, find, 0)
        top = jnp.max(mx[...], axis=1, keepdims=True)
        mx[...] = jnp.broadcast_to(top, (QROWS, 128))
        den[...] = jnp.zeros_like(den)
        acc[...] = jnp.zeros_like(acc)

        def blend(i, carry):
            weights = jnp.exp2((sbuf[i] - mx[:, 0:1]) * FACTOR)
            den[...] += fold(weights, jnp.add)
            acc[...] += jnp.dot(
                weights.astype(jnp.bfloat16), kv[chunk_rows(i), HEAD_SIZE:], preferred_element_type=jnp.float32
            )
            return carry

        lax.fori_loop(0, z + 1, blend, 0)
        total = jnp.sum(den[...], axis=1, keepdims=True)
        done = (acc[...] / total).astype(jnp.bfloat16)
        for g in range(GROUP):
            stage[p, :, g * HEAD_SIZE : (g + 1) * HEAD_SIZE] = done[g * TOK_W : (g + 1) * TOK_W, :]

        @pl.when(d < N_HEAD)
        def _():
            remote(stage.at[p], out_ref.at[:, wide(h)], o_s.at[d], o_r.at[d], head=p).start()

        return carry

    lax.fori_loop(1, N_HEAD + 1, tile, 0)
    last = pltpu.make_async_copy(stage.at[h], out_ref.at[:, wide(h)], own_sem.at[0])
    last.start()
    last.wait()
    for c in first + queries:
        c.wait_send()
    for way in range(2):
        for t in range(4):
            for c in steps[way][t]:
                c.wait_send()
    for d in range(1, N_HEAD):
        p = lax.rem(h + d, N_HEAD)
        remote(stage.at[p], out_ref.at[:, wide(h)], o_s.at[d], o_r.at[d], head=p).wait()


def body(queries, keys, values, counts, offsets, tree_ids, block_lists):
    any_space = pl.BlockSpec(memory_space=pl.ANY)
    smem = pl.BlockSpec(memory_space=pltpu.SMEM)
    dma = pltpu.SemaphoreType.DMA
    return pl.pallas_call(
        kernel,
        out_shape=jax.ShapeDtypeStruct((TOK_W, KEY_VALUE_HEADS * WIDE), jnp.bfloat16),
        in_specs=[smem] * 4 + [any_space] * 3,
        out_specs=any_space,
        scratch_shapes=[
            pltpu.VMEM((N_HEAD, TOK_W, WIDE), jnp.bfloat16),
            pltpu.VMEM((N_SEQ * ROW, 2 * HEAD_SIZE), jnp.bfloat16),
            pltpu.VMEM((N_SEQ * ROW, 128), jnp.bfloat16),
            pltpu.VMEM((N_SEQ, N_HEAD, 1, 128), jnp.float32),
            pltpu.VMEM((N_SEQ, QB, 1, 128), jnp.float32),
            pltpu.VMEM((QROWS, 2 * HEAD_SIZE), jnp.bfloat16),
            pltpu.VMEM((N_SEQ, QROWS, ROW), jnp.float32),
            pltpu.VMEM((QROWS, 128), jnp.float32),
            pltpu.VMEM((QROWS, 128), jnp.float32),
            pltpu.VMEM((QROWS, HEAD_SIZE), jnp.float32),
            pltpu.VMEM((N_HEAD, TOK_W, WIDE), jnp.bfloat16),
            dma((3,)),
            dma((N_HEAD, 2)),
            dma((N_HEAD, 2)),
            dma((N_HEAD,)),
            dma((N_HEAD,)),
            dma((N_HEAD,)),
            dma((N_HEAD,)),
            dma((2, 4, 2)),
            dma((2, 4, 2)),
            dma((2, 4)),
            dma((2, 4)),
            dma((2, 4)),
            dma((2, 4)),
            dma((N_HEAD + 1,)),
            dma((N_HEAD + 1,)),
        ],
        compiler_params=pltpu.CompilerParams(
            collective_id=0, has_side_effects=True, vmem_limit_bytes=48 * 1024 * 1024
        ),
    )(counts, offsets, tree_ids, block_lists, queries, keys, values)


def solution(mesh):
    split = P(("rep", "seq", "head"), None)
    placed = (split,) * 6 + (P(("rep", "seq"), None, None),)
    return jax.shard_map(body, mesh=mesh, in_specs=placed, out_specs=split, check_vma=False)
```

```python
import math

import jax
import jax.numpy as jnp
from jax import lax
from jax.experimental import pallas as pl
from jax.experimental.pallas import tpu as pltpu
from jax.sharding import PartitionSpec as P

MESH = pl.DeviceIdType.MESH
KEY_VALUE_HEADS = 8
GROUP = 8
HEAD_SIZE = 128
TOK_W = 64
SLOT = 32
ANCESTOR_COUNT = 7
QB = 16
N_SEQ = 8
N_HEAD = 8
ROW = N_HEAD * TOK_W
HALF = ROW // 2
WIDE = GROUP * HEAD_SIZE
TILE = GROUP * SLOT
QROWS = N_HEAD * TILE
PIECE = 2 * TOK_W
ORDER = (0, 1, 3, 2)
NEG = -1e30
FACTOR = math.log2(math.e) / math.sqrt(HEAD_SIZE)
NT = (((1,), (1,)), ((), ()))
BF16 = jnp.bfloat16
F32 = jnp.float32


def kernel(
    cnt_ref, off_ref, tree_ref, bl_ref, q_ref, k_ref, v_ref, out_ref,
    qbuf, kv, ks, vs, ids, anc, qa, sbuf, mx, den, acc, osort, stage,
    own_sem, kv_s, kv_r, id_s, id_r, q_s, q_r, ring_s, ring_r, idr_s, idr_r, an_s, an_r, o_s, o_r,
):
    z = lax.axis_index("seq")
    h = lax.axis_index("head")
    up = lax.rem(z + 1, N_SEQ)
    down = lax.rem(z + N_SEQ - 1, N_SEQ)

    barrier = pltpu.get_barrier_semaphore()
    for d in range(1, N_HEAD):
        pl.semaphore_signal(barrier, inc=1, device_id={"head": lax.rem(h + d, N_HEAD)}, device_id_type=MESH)
    for d in range(1, N_SEQ):
        pl.semaphore_signal(barrier, inc=1, device_id={"seq": lax.rem(z + d, N_SEQ)}, device_id_type=MESH)

    def cols(p):
        return pl.ds(pl.multiple_of(p * HEAD_SIZE, HEAD_SIZE), HEAD_SIZE)

    def wide(p):
        return pl.ds(pl.multiple_of(p * WIDE, WIDE), WIDE)

    mine = pl.ds(pl.multiple_of(z * ROW + h * TOK_W, TOK_W), TOK_W)
    left, right = pl.ds(0, HEAD_SIZE), pl.ds(HEAD_SIZE, HEAD_SIZE)
    own = [
        pltpu.make_async_copy(k_ref.at[:, cols(h)], kv.at[mine, left], own_sem.at[0]),
        pltpu.make_async_copy(v_ref.at[:, cols(h)], kv.at[mine, right], own_sem.at[1]),
        pltpu.make_async_copy(q_ref.at[:, wide(h)], qbuf.at[h], own_sem.at[2]),
    ]
    for c in own:
        c.start()

    lane1 = lax.broadcasted_iota(jnp.int32, (1, 128), 1)
    info = jnp.zeros((1, 128), F32)
    for s in range(N_SEQ):
        start, count = off_ref[0, s], cnt_ref[0, s]
        member = (lane1 >= start) & (lane1 < start + count)
        info = jnp.where(member, (s * 4 + tree_ref[0, s]).astype(F32), info)
        info = jnp.where(lane1 == TOK_W + s, count.astype(F32), info)
        info = jnp.where(lane1 == TOK_W + N_SEQ + s, start.astype(F32), info)
    ids[z, h] = info
    lane_block = (lane1 - 32) >> 2
    for b in range(QB):
        hit = jnp.zeros((1, 128), F32)
        for k in range(ANCESTOR_COUNT):
            e = bl_ref[k, 0, b]
            hit = jnp.where((lane_block == e) & (lane1 >= 32), 1.0, hit)
        anc[z, b] = hit

    pl.semaphore_wait(barrier, N_HEAD + N_SEQ - 2)

    def remote(src, dst, s_sem, r_sem, **where):
        return pltpu.make_async_remote_copy(
            src_ref=src, dst_ref=dst, send_sem=s_sem, recv_sem=r_sem, device_id=where, device_id_type=MESH
        )

    others = [lax.rem(h + d, N_HEAD) for d in range(N_HEAD)]
    id_row = [remote(ids.at[z, h], ids.at[z, h], id_s.at[d], id_r.at[d], head=others[d]) for d in range(1, N_HEAD)]
    k_row = [
        remote(k_ref.at[:, cols(others[d])], kv.at[mine, left], kv_s.at[d, 0], kv_r.at[d, 0], head=others[d])
        for d in range(1, N_HEAD)
    ]
    v_row = [
        remote(v_ref.at[:, cols(others[d])], kv.at[mine, right], kv_s.at[d, 1], kv_r.at[d, 1], head=others[d])
        for d in range(1, N_HEAD)
    ]
    q_row = [
        remote(q_ref.at[:, wide(others[d])], qbuf.at[h], q_s.at[d], q_r.at[d], head=others[d])
        for d in range(1, N_HEAD)
    ]
    for c in id_row:
        c.start()
    for a, b in zip(k_row, v_row):
        a.start()
        b.start()

    chip = h // 2

    def piece(r, j):
        c = lax.rem(chip + ORDER[j], 4)
        return kv.at[pl.ds(pl.multiple_of(r * ROW + c * PIECE, PIECE), PIECE)]

    def source(way, t):
        return lax.rem(z + N_SEQ - t, N_SEQ) if way == 0 else lax.rem(z + t, N_SEQ)

    def hop(way, t, j):
        ref = piece(source(way, t), j)
        return remote(ref, ref, ring_s.at[way, t, j], ring_r.at[way, t, j], seq=up if way == 0 else down)

    def pieces(way, t):
        return range(4) if t < 3 else (range(2) if way == 0 else range(2, 4))

    ring = {(way, t, j): hop(way, t, j) for way in range(2) for t in range(4) for j in pieces(way, t)}

    def landed(j):
        for q in range(2):
            src = lax.rem(chip + ORDER[j], 4) * 2 + q
            d = lax.rem(h + N_HEAD - src, N_HEAD)

            @pl.when(d == 0)
            def _():
                own[0].wait()
                own[1].wait()

            @pl.when(d != 0)
            def _():
                remote(kv.at[mine, left], kv.at[mine, left], kv_s.at[d, 0], kv_r.at[d, 0], head=src).wait_recv()
                remote(kv.at[mine, right], kv.at[mine, right], kv_s.at[d, 1], kv_r.at[d, 1], head=src).wait_recv()

    for j in range(4):
        landed(j)
        for way in range(2):
            ring[way, 0, j].start()
        if j == 0:
            for c in q_row:
                c.start()
        if j == 1:
            for c in id_row:
                c.wait_recv()
            id_col, an_col = [], []
            for e in range(1, N_SEQ):
                to = lax.rem(z + e, N_SEQ)
                id_col.append(remote(ids.at[z], ids.at[z], idr_s.at[e], idr_r.at[e], seq=to))
                two = pl.ds(2 * to, 2)
                an_col.append(remote(anc.at[z, two], anc.at[z, two], an_s.at[e], an_r.at[e], seq=to))
            for c in id_col + an_col:
                c.start()

    for c in id_col + an_col:
        c.wait_recv()
    least = jnp.full((1, 128), 1e9, F32)
    for r in range(N_SEQ):
        for w in range(N_HEAD):
            least = jnp.minimum(least, ids[r, w])
    lane1f = lane1.astype(F32)
    is_full = (lane1 >= TOK_W) & (lane1 < TOK_W + N_SEQ) & (least > SLOT - 0.5)
    full = jnp.min(jnp.where(is_full, lane1f, 1e9), axis=1, keepdims=True)

    def first_row(r, w):
        return jnp.sum(jnp.where(lane1f == full + N_SEQ, ids[r, w], 0.0), axis=1, keepdims=True)

    lane = lax.broadcasted_iota(jnp.int32, (TOK_W, 128), 1)
    tok = lax.broadcasted_iota(jnp.int32, (TOK_W, 128), 0)

    def column(row):
        return jnp.sum(jnp.where(lane == tok, row, 0.0), axis=1, keepdims=True)

    FOUR = 4 * TOK_W
    r4 = lax.broadcasted_iota(jnp.int32, (FOUR, 1), 0)
    c4 = lax.broadcasted_iota(jnp.int32, (FOUR, FOUR), 1).astype(F32)
    who4, place4 = (r4 >> 5) & 3, ((r4 >> 7) * SLOT + (r4 & (SLOT - 1))).astype(F32)

    def sort_keys(r):
        for u in range(2):
            begin = jnp.zeros((FOUR, 1), F32)
            parts = []
            for n in range(4):
                w = 4 * u + n
                begin = jnp.where(who4 == n, first_row(r, w), begin)
                hot = (lane.astype(F32) == column(ids[r, w])) | (lane == 32 + r * N_HEAD + w)
                parts.append(jnp.where(hot, 1.0, 0.0).astype(BF16))
            t = begin + place4
            t = jnp.where(t >= TOK_W, t - TOK_W, t) + (who4 * TOK_W).astype(F32)
            move = jnp.where(c4 == t, 1.0, 0.0).astype(BF16)
            rows = pl.ds(pl.multiple_of(r * ROW + u * FOUR, FOUR), FOUR)
            both = jnp.dot(move, kv[rows, :], preferred_element_type=F32).astype(BF16)
            marks = jnp.dot(move, jnp.concatenate(parts, axis=0), preferred_element_type=F32).astype(BF16)
            here = pl.ds(u * 128, 128)
            for f in range(2):
                ks[f, r, here, 0:HEAD_SIZE] = both[f * 128 : (f + 1) * 128, 0:HEAD_SIZE]
                ks[f, r, here, HEAD_SIZE:] = marks[f * 128 : (f + 1) * 128]
                vs[f, r, here, :] = both[f * 128 : (f + 1) * 128, HEAD_SIZE:]

    c1 = lax.broadcasted_iota(jnp.int32, (TOK_W, TOK_W), 1).astype(F32)
    r1 = lax.broadcasted_iota(jnp.int32, (TOK_W, TOK_W), 0).astype(F32)

    def prepare_queries(p, carry):
        w = z * N_HEAD + p
        b = w // 4
        c = column(ids[z, p])
        shard = jnp.floor(c * 0.25)
        looks = jnp.zeros((TOK_W, 128), F32)
        for s in range(N_SEQ):
            looks = jnp.where(shard == float(s), anc[s, b], looks)
        worker = lane - 32
        own_block = ((worker >> 2) == b) & (worker <= w)
        fine = jnp.where(
            lane < 32,
            jnp.where(lane.astype(F32) == c, 1.0, 0.0),
            jnp.where((lane >= 96) | own_block, 1.0, looks),
        )
        penalty = jnp.where(fine > 0.5, 0.0, NEG).astype(BF16)
        t = first_row(z, p) + r1
        t = jnp.where(t >= TOK_W, t - TOK_W, t)
        move = jnp.where(c1 == t, 1.0, 0.0).astype(BF16)
        rows = jnp.dot(move, qbuf[p], preferred_element_type=F32).astype(BF16)
        marks = jnp.dot(move, penalty, preferred_element_type=F32).astype(BF16)
        for f in range(2):
            part = slice(f * SLOT, (f + 1) * SLOT)
            for g in range(GROUP):
                to = pl.ds(pl.multiple_of(p * TILE + g * SLOT, SLOT), SLOT)
                qa[f, to, 0:HEAD_SIZE] = rows[part, g * HEAD_SIZE : (g + 1) * HEAD_SIZE]
                qa[f, to, HEAD_SIZE:] = marks[part]
        return carry

    BLOCK = 512
    row_id = lax.broadcasted_iota(jnp.int32, (BLOCK, HALF), 0)
    col_id = lax.broadcasted_iota(jnp.int32, (BLOCK, HALF), 1)
    late_pos = (col_id & (SLOT - 1)) > (row_id & (SLOT - 1))

    def score(r, f, is_own):
        def block(n, carry):
            at = pl.ds(pl.multiple_of(n * BLOCK, BLOCK), BLOCK)
            s = lax.dot_general(qa[f, at, :], ks[f, r], NT, preferred_element_type=F32) * FACTOR
            if is_own:
                late = late_pos & ((col_id >> 5) == (row_id >> 8) + n * (BLOCK // TILE))
                s = jnp.where(late, NEG, s)
            sbuf[f, r, at, :] = s
            top = jnp.maximum(s[:, 0:128], s[:, 128:])
            mx[f, at, :] = top if is_own else jnp.maximum(mx[f, at, :], top)
            return carry

        lax.fori_loop(0, QROWS // BLOCK, block, 0)

    def sort_if(r):
        @pl.when(r <= z)
        def _():
            sort_keys(r)

    def score_if(r):
        @pl.when(r <= z)
        def _():
            for f in range(2):
                score(r, f, False)

    def forward(t, j):
        for way in range(2):
            if (way, t - 1, j) in ring:
                ring[way, t - 1, j].wait_recv()
            if (way, t, j) in ring:
                ring[way, t, j].start()

    def ready_queries():
        own[2].wait()
        for c in q_row:
            c.wait_recv()
        lax.fori_loop(0, N_HEAD, prepare_queries, 0)

    near = {(way, t): source(way, t) for way in range(2) for t in range(1, 4)}
    opposite = lax.rem(z + 4, N_SEQ)
    sort_keys(z)
    for j in range(4):
        forward(1, j)
    forward(2, 0)
    sort_if(near[0, 1])
    forward(2, 1)
    sort_if(near[1, 1])
    forward(2, 2)
    forward(2, 3)
    ready_queries()
    forward(3, 0)
    forward(3, 1)
    sort_if(near[0, 2])
    score(z, 0, True)
    score(z, 1, True)
    forward(3, 2)
    forward(3, 3)
    sort_if(near[1, 2])
    for way in range(2):
        score_if(near[way, 1])
        score_if(near[way, 2])
    sort_if(near[0, 3])
    sort_if(near[1, 3])
    for way in range(2):
        score_if(near[way, 3])
    for j in range(4):
        forward(4, j)
    sort_if(opposite)
    score_if(opposite)

    def tile(d, carry):
        p = lax.rem(h + d, N_HEAD)
        at = pl.ds(pl.multiple_of(p * TILE, TILE), TILE)
        for f in range(2):
            top = jnp.max(mx[f, at, :], axis=1, keepdims=True)
            mx[f, at, :] = jnp.broadcast_to(top, (TILE, 128))
            den[f] = jnp.zeros((TILE, 128), F32)
            acc[f] = jnp.zeros((TILE, HEAD_SIZE), F32)

        def blend(i, carry):
            for f in range(2):
                top = mx[f, at, :]
                weights = jnp.exp2(sbuf[f, i, at, :] - jnp.concatenate([top, top], axis=1))
                den[f] += weights[:, 0:128] + weights[:, 128:]
                acc[f] += jnp.dot(weights.astype(BF16), vs[f, i], preferred_element_type=F32)
            return carry

        lax.fori_loop(0, z + 1, blend, 0)
        for f in range(2):
            total = jnp.sum(den[f], axis=1, keepdims=True)
            done = (acc[f] / total).astype(BF16)
            for g in range(GROUP):
                osort[f * SLOT : (f + 1) * SLOT, g * HEAD_SIZE : (g + 1) * HEAD_SIZE] = done[
                    g * SLOT : (g + 1) * SLOT
                ]
        t = r1 - first_row(z, p)
        t = jnp.where(t < 0.0, t + TOK_W, t)
        back = jnp.where(c1 == t, 1.0, 0.0).astype(BF16)
        stage[p] = jnp.dot(back, osort[...], preferred_element_type=F32).astype(BF16)

        @pl.when(d < N_HEAD)
        def _():
            remote(stage.at[p], out_ref.at[:, wide(h)], o_s.at[d], o_r.at[d], head=p).start()

        return carry

    lax.fori_loop(1, N_HEAD + 1, tile, 0)
    last = pltpu.make_async_copy(stage.at[h], out_ref.at[:, wide(h)], own_sem.at[0])
    last.start()
    last.wait()
    for c in id_row + k_row + v_row + q_row + id_col + an_col + list(ring.values()):
        c.wait_send()
    for d in range(1, N_HEAD):
        p = lax.rem(h + d, N_HEAD)
        remote(stage.at[p], out_ref.at[:, wide(h)], o_s.at[d], o_r.at[d], head=p).wait()


def body(queries, keys, values, counts, offsets, tree_ids, block_lists):
    any_space = pl.BlockSpec(memory_space=pl.ANY)
    smem = pl.BlockSpec(memory_space=pltpu.SMEM)
    dma = pltpu.SemaphoreType.DMA
    return pl.pallas_call(
        kernel,
        out_shape=jax.ShapeDtypeStruct((TOK_W, KEY_VALUE_HEADS * WIDE), BF16),
        in_specs=[smem] * 4 + [any_space] * 3,
        out_specs=any_space,
        scratch_shapes=[
            pltpu.VMEM((N_HEAD, TOK_W, WIDE), BF16),
            pltpu.VMEM((N_SEQ * ROW, 2 * HEAD_SIZE), BF16),
            pltpu.VMEM((2, N_SEQ, HALF, 2 * HEAD_SIZE), BF16),
            pltpu.VMEM((2, N_SEQ, HALF, HEAD_SIZE), BF16),
            pltpu.VMEM((N_SEQ, N_HEAD, 1, 128), F32),
            pltpu.VMEM((N_SEQ, QB, 1, 128), F32),
            pltpu.VMEM((2, QROWS, 2 * HEAD_SIZE), BF16),
            pltpu.VMEM((2, N_SEQ, QROWS, HALF), F32),
            pltpu.VMEM((2, QROWS, 128), F32),
            pltpu.VMEM((2, TILE, 128), F32),
            pltpu.VMEM((2, TILE, HEAD_SIZE), F32),
            pltpu.VMEM((TOK_W, WIDE), BF16),
            pltpu.VMEM((N_HEAD, TOK_W, WIDE), BF16),
            dma((3,)),
            dma((N_HEAD, 2)),
            dma((N_HEAD, 2)),
            dma((N_HEAD,)),
            dma((N_HEAD,)),
            dma((N_HEAD,)),
            dma((N_HEAD,)),
            dma((2, 4, 4)),
            dma((2, 4, 4)),
            dma((N_SEQ,)),
            dma((N_SEQ,)),
            dma((N_SEQ,)),
            dma((N_SEQ,)),
            dma((N_HEAD + 1,)),
            dma((N_HEAD + 1,)),
        ],
        compiler_params=pltpu.CompilerParams(
            collective_id=0, has_side_effects=True, vmem_limit_bytes=62 * 1024 * 1024
        ),
    )(counts, offsets, tree_ids, jnp.transpose(block_lists, (2, 0, 1)), queries, keys, values)


def solution(mesh):
    split = P(("rep", "seq", "head"), None)
    placed = (split,) * 6 + (P(("rep", "seq"), None, None),)
    return jax.shard_map(body, mesh=mesh, in_specs=placed, out_specs=split, check_vma=False)
```

```python
import functools
import math

import jax
import jax.numpy as jnp
from jax import lax
from jax.experimental import pallas as pl
from jax.experimental.pallas import tpu as pltpu
from jax.sharding import PartitionSpec as P

MESH = pl.DeviceIdType.MESH
KEY_VALUE_HEADS = 8
GROUP = 8
HEAD_SIZE = 128
TOK_W = 64
SLOT = 32
ANCESTOR_COUNT = 7
QB = 16
N_SEQ = 8
N_HEAD = 8
ROW = N_HEAD * TOK_W
HALF = ROW // 2
WIDE = GROUP * HEAD_SIZE
TILE = GROUP * SLOT
QROWS = N_HEAD * TILE
PIECE = 2 * TOK_W
ORDER = (0, 1, 3, 2)
NEG = -1e30
FACTOR = math.log2(math.e) / math.sqrt(HEAD_SIZE)
NT = (((1,), (1,)), ((), ()))
BF16 = jnp.bfloat16
F32 = jnp.float32


def kernel(
    cnt_ref, off_ref, tree_ref, bl_ref, q_ref, k_ref, v_ref, out_ref,
    qbuf, kv, ks, vs, ids, anc, qa, sbuf, mx, osort, stage,
    own_sem, kv_s, kv_r, id_s, id_r, q_s, q_r, ring_s, ring_r, idr_s, idr_r, an_s, an_r, o_s, o_r,
):
    z = lax.axis_index("seq")
    h = lax.axis_index("head")
    up = lax.rem(z + 1, N_SEQ)
    down = lax.rem(z + N_SEQ - 1, N_SEQ)

    barrier = pltpu.get_barrier_semaphore()
    for d in range(1, N_HEAD):
        pl.semaphore_signal(barrier, inc=1, device_id={"head": lax.rem(h + d, N_HEAD)}, device_id_type=MESH)
    for d in range(1, N_SEQ):
        pl.semaphore_signal(barrier, inc=1, device_id={"seq": lax.rem(z + d, N_SEQ)}, device_id_type=MESH)

    def cols(p):
        return pl.ds(pl.multiple_of(p * HEAD_SIZE, HEAD_SIZE), HEAD_SIZE)

    def wide(p):
        return pl.ds(pl.multiple_of(p * WIDE, WIDE), WIDE)

    mine = pl.ds(pl.multiple_of(z * ROW + h * TOK_W, TOK_W), TOK_W)
    left, right = pl.ds(0, HEAD_SIZE), pl.ds(HEAD_SIZE, HEAD_SIZE)
    own = [
        pltpu.make_async_copy(k_ref.at[:, cols(h)], kv.at[mine, left], own_sem.at[0]),
        pltpu.make_async_copy(v_ref.at[:, cols(h)], kv.at[mine, right], own_sem.at[1]),
        pltpu.make_async_copy(q_ref.at[:, wide(h)], qbuf.at[h], own_sem.at[2]),
    ]
    for c in own:
        c.start()

    lane1 = lax.broadcasted_iota(jnp.int32, (1, 128), 1)
    info = jnp.zeros((1, 128), F32)
    for s in range(N_SEQ):
        start, count = off_ref[0, s], cnt_ref[0, s]
        member = (lane1 >= start) & (lane1 < start + count)
        info = jnp.where(member, (s * 4 + tree_ref[0, s]).astype(F32), info)
        info = jnp.where(lane1 == TOK_W + s, count.astype(F32), info)
        info = jnp.where(lane1 == TOK_W + N_SEQ + s, start.astype(F32), info)
    ids[z, h] = info
    lane_block = (lane1 - 32) >> 2
    for b in range(QB):
        hit = jnp.zeros((1, 128), F32)
        for k in range(ANCESTOR_COUNT):
            e = bl_ref[k, 0, b]
            hit = jnp.where((lane_block == e) & (lane1 >= 32), 1.0, hit)
        anc[z, b] = hit

    pl.semaphore_wait(barrier, N_HEAD + N_SEQ - 2)

    def remote(src, dst, s_sem, r_sem, **where):
        return pltpu.make_async_remote_copy(
            src_ref=src, dst_ref=dst, send_sem=s_sem, recv_sem=r_sem, device_id=where, device_id_type=MESH
        )

    others = [lax.rem(h + d, N_HEAD) for d in range(N_HEAD)]
    id_row = [remote(ids.at[z, h], ids.at[z, h], id_s.at[d], id_r.at[d], head=others[d]) for d in range(1, N_HEAD)]
    k_row = [
        remote(k_ref.at[:, cols(others[d])], kv.at[mine, left], kv_s.at[d, 0], kv_r.at[d, 0], head=others[d])
        for d in range(1, N_HEAD)
    ]
    v_row = [
        remote(v_ref.at[:, cols(others[d])], kv.at[mine, right], kv_s.at[d, 1], kv_r.at[d, 1], head=others[d])
        for d in range(1, N_HEAD)
    ]
    q_row = [
        remote(q_ref.at[:, wide(others[d])], qbuf.at[h], q_s.at[d], q_r.at[d], head=others[d])
        for d in range(1, N_HEAD)
    ]
    for c in id_row:
        c.start()
    for a, b in zip(k_row, v_row):
        a.start()
        b.start()

    chip = h // 2

    def piece(r, j):
        c = lax.rem(chip + ORDER[j], 4)
        return kv.at[pl.ds(pl.multiple_of(r * ROW + c * PIECE, PIECE), PIECE)]

    def source(way, t):
        return lax.rem(z + N_SEQ - t, N_SEQ) if way == 0 else lax.rem(z + t, N_SEQ)

    def hop(way, t, j):
        ref = piece(source(way, t), j)
        return remote(ref, ref, ring_s.at[way, t, j], ring_r.at[way, t, j], seq=up if way == 0 else down)

    def pieces(way, t):
        return range(4) if t < 3 else (range(2) if way == 0 else range(2, 4))

    ring = {(way, t, j): hop(way, t, j) for way in range(2) for t in range(4) for j in pieces(way, t)}

    def landed(j):
        for q in range(2):
            src = lax.rem(chip + ORDER[j], 4) * 2 + q
            d = lax.rem(h + N_HEAD - src, N_HEAD)

            @pl.when(d == 0)
            def _():
                own[0].wait()
                own[1].wait()

            @pl.when(d != 0)
            def _():
                remote(kv.at[mine, left], kv.at[mine, left], kv_s.at[d, 0], kv_r.at[d, 0], head=src).wait_recv()
                remote(kv.at[mine, right], kv.at[mine, right], kv_s.at[d, 1], kv_r.at[d, 1], head=src).wait_recv()

    for j in range(4):
        landed(j)
        for way in range(2):
            ring[way, 0, j].start()
        if j == 0:
            for c in q_row:
                c.start()
        if j == 1:
            for c in id_row:
                c.wait_recv()
            id_col, an_col = [], []
            for e in range(1, N_SEQ):
                to = lax.rem(z + e, N_SEQ)
                id_col.append(remote(ids.at[z], ids.at[z], idr_s.at[e], idr_r.at[e], seq=to))
                two = pl.ds(2 * to, 2)
                an_col.append(remote(anc.at[z, two], anc.at[z, two], an_s.at[e], an_r.at[e], seq=to))
            for c in id_col + an_col:
                c.start()

    for c in id_col + an_col:
        c.wait_recv()
    least = jnp.full((1, 128), 1e9, F32)
    for r in range(N_SEQ):
        for w in range(N_HEAD):
            least = jnp.minimum(least, ids[r, w])
    lane1f = lane1.astype(F32)
    is_full = (lane1 >= TOK_W) & (lane1 < TOK_W + N_SEQ) & (least > SLOT - 0.5)
    full = jnp.min(jnp.where(is_full, lane1f, 1e9), axis=1, keepdims=True)

    def first_row(r, w):
        return jnp.sum(jnp.where(lane1f == full + N_SEQ, ids[r, w], 0.0), axis=1, keepdims=True)

    lane = lax.broadcasted_iota(jnp.int32, (TOK_W, 128), 1)
    tok = lax.broadcasted_iota(jnp.int32, (TOK_W, 128), 0)

    def column(row):
        return jnp.sum(jnp.where(lane == tok, row, 0.0), axis=1, keepdims=True)

    FOUR = 4 * TOK_W
    r4 = lax.broadcasted_iota(jnp.int32, (FOUR, 1), 0)
    c4 = lax.broadcasted_iota(jnp.int32, (FOUR, FOUR), 1).astype(F32)
    who4, place4 = (r4 >> 5) & 3, ((r4 >> 7) * SLOT + (r4 & (SLOT - 1))).astype(F32)

    def sort_keys(r):
        for u in range(2):
            begin = jnp.zeros((FOUR, 1), F32)
            parts = []
            for n in range(4):
                w = 4 * u + n
                begin = jnp.where(who4 == n, first_row(r, w), begin)
                hot = (lane.astype(F32) == column(ids[r, w])) | (lane == 32 + r * N_HEAD + w)
                parts.append(jnp.where(hot, 1.0, 0.0).astype(BF16))
            t = begin + place4
            t = jnp.where(t >= TOK_W, t - TOK_W, t) + (who4 * TOK_W).astype(F32)
            move = jnp.where(c4 == t, 1.0, 0.0).astype(BF16)
            rows = pl.ds(pl.multiple_of(r * ROW + u * FOUR, FOUR), FOUR)
            both = jnp.dot(move, kv[rows, :], preferred_element_type=F32).astype(BF16)
            marks = jnp.dot(move, jnp.concatenate(parts, axis=0), preferred_element_type=F32).astype(BF16)
            here = pl.ds(u * 128, 128)
            for f in range(2):
                ks[f, r, here, 0:HEAD_SIZE] = both[f * 128 : (f + 1) * 128, 0:HEAD_SIZE]
                ks[f, r, here, HEAD_SIZE:] = marks[f * 128 : (f + 1) * 128]
                vs[f, pl.ds(pl.multiple_of(r * HALF + u * 128, 128), 128), :] = both[f * 128 : (f + 1) * 128, HEAD_SIZE:]

    c1 = lax.broadcasted_iota(jnp.int32, (TOK_W, TOK_W), 1).astype(F32)
    r1 = lax.broadcasted_iota(jnp.int32, (TOK_W, TOK_W), 0).astype(F32)

    def prepare_queries(p, carry):
        w = z * N_HEAD + p
        b = w // 4
        c = column(ids[z, p])
        shard = jnp.floor(c * 0.25)
        looks = jnp.zeros((TOK_W, 128), F32)
        for s in range(N_SEQ):
            looks = jnp.where(shard == float(s), anc[s, b], looks)
        worker = lane - 32
        own_block = ((worker >> 2) == b) & (worker <= w)
        fine = jnp.where(
            lane < 32,
            jnp.where(lane.astype(F32) == c, 1.0, 0.0),
            jnp.where((lane >= 96) | own_block, 1.0, looks),
        )
        penalty = jnp.where(fine > 0.5, 0.0, NEG).astype(BF16)
        t = first_row(z, p) + r1
        t = jnp.where(t >= TOK_W, t - TOK_W, t)
        move = jnp.where(c1 == t, 1.0, 0.0).astype(BF16)
        rows = jnp.dot(move, qbuf[p], preferred_element_type=F32).astype(BF16)
        marks = jnp.dot(move, penalty, preferred_element_type=F32).astype(BF16)
        for f in range(2):
            part = slice(f * SLOT, (f + 1) * SLOT)
            for g in range(GROUP):
                to = pl.ds(pl.multiple_of(p * TILE + g * SLOT, SLOT), SLOT)
                qa[f, to, 0:HEAD_SIZE] = rows[part, g * HEAD_SIZE : (g + 1) * HEAD_SIZE]
                qa[f, to, HEAD_SIZE:] = marks[part]
        return carry

    BLOCK = 2048
    row_id = lax.broadcasted_iota(jnp.int32, (BLOCK, HALF), 0)
    col_id = lax.broadcasted_iota(jnp.int32, (BLOCK, HALF), 1)
    late_pos = (col_id & (SLOT - 1)) > (row_id & (SLOT - 1))

    def score(r, f, is_own):
        def block(n, carry):
            at = pl.ds(pl.multiple_of(n * BLOCK, BLOCK), BLOCK)
            s = lax.dot_general(qa[f, at, :], ks[f, r], NT, preferred_element_type=F32) * FACTOR
            if is_own:
                late = late_pos & ((col_id >> 5) == (row_id >> 8) + n * (BLOCK // TILE))
                s = jnp.where(late, NEG, s)
            sbuf[f, at, pl.ds(pl.multiple_of(r * HALF, HALF), HALF)] = s
            top = jnp.maximum(s[:, 0:128], s[:, 128:])
            mx[f, at, :] = top if is_own else jnp.maximum(mx[f, at, :], top)
            return carry

        lax.fori_loop(0, QROWS // BLOCK, block, 0)

    def sort_if(r):
        @pl.when(r < bound)
        def _():
            sort_keys(r)

    def score_if(r):
        @pl.when(r < bound)
        def _():
            for f in range(2):
                score(r, f, False)

    def forward(t, j):
        for way in range(2):
            if (way, t - 1, j) in ring:
                ring[way, t - 1, j].wait_recv()
            if (way, t, j) in ring:
                ring[way, t, j].start()

    def ready_queries():
        own[2].wait()
        for c in q_row:
            c.wait_recv()
        lax.fori_loop(0, N_HEAD, prepare_queries, 0)

    bound = jnp.where(z < N_SEQ // 2, N_SEQ // 2, N_SEQ)
    near = {(way, t): source(way, t) for way in range(2) for t in range(1, 4)}
    opposite = lax.rem(z + 4, N_SEQ)
    sort_keys(z)
    for j in range(4):
        forward(1, j)
    forward(2, 0)
    sort_if(near[0, 1])
    forward(2, 1)
    sort_if(near[1, 1])
    forward(2, 2)
    forward(2, 3)
    forward(3, 0)
    sort_if(near[0, 2])
    forward(3, 1)
    sort_if(near[1, 2])
    ready_queries()
    forward(3, 2)
    score(z, 0, True)
    score(z, 1, True)
    forward(3, 3)
    score_if(near[0, 1])
    score_if(near[1, 1])
    forward(4, 0)
    forward(4, 2)
    score_if(near[0, 2])
    score_if(near[1, 2])
    for way in range(2):
        sort_if(near[way, 3])
        score_if(near[way, 3])
    forward(4, 1)
    forward(4, 3)
    sort_if(opposite)
    score_if(opposite)

    def tile(limit, d, carry):
        p = lax.rem(h + d, N_HEAD)
        at = pl.ds(pl.multiple_of(p * TILE, TILE), TILE)
        keys = limit * HALF
        for f in range(2):
            top = jnp.broadcast_to(jnp.max(mx[f, at, :], axis=1, keepdims=True), (TILE, 128))
            weights = jnp.exp2(sbuf[f, at, 0:keys] - jnp.concatenate([top] * (keys // 128), axis=1))
            total = weights[:, 0:128]
            for n in range(1, keys // 128):
                total = total + weights[:, n * 128 : (n + 1) * 128]
            blend = jnp.dot(weights.astype(BF16), vs[f, 0:keys, :], preferred_element_type=F32)
            done = (blend / jnp.sum(total, axis=1, keepdims=True)).astype(BF16)
            for g in range(GROUP):
                osort[f * SLOT : (f + 1) * SLOT, g * HEAD_SIZE : (g + 1) * HEAD_SIZE] = done[
                    g * SLOT : (g + 1) * SLOT
                ]
        t = r1 - first_row(z, p)
        t = jnp.where(t < 0.0, t + TOK_W, t)
        back = jnp.where(c1 == t, 1.0, 0.0).astype(BF16)
        stage[p] = jnp.dot(back, osort[...], preferred_element_type=F32).astype(BF16)

        @pl.when(d < N_HEAD)
        def _():
            remote(stage.at[p], out_ref.at[:, wide(h)], o_s.at[d], o_r.at[d], head=p).start()

        return carry

    for limit in (N_SEQ // 2, N_SEQ):

        @pl.when(bound == limit)
        def _():
            lax.fori_loop(1, N_HEAD + 1, functools.partial(tile, limit), 0)

    last = pltpu.make_async_copy(stage.at[h], out_ref.at[:, wide(h)], own_sem.at[0])
    last.start()
    last.wait()
    for c in id_row + k_row + v_row + q_row + id_col + an_col + list(ring.values()):
        c.wait_send()
    for d in range(1, N_HEAD):
        p = lax.rem(h + d, N_HEAD)
        remote(stage.at[p], out_ref.at[:, wide(h)], o_s.at[d], o_r.at[d], head=p).wait()


def body(queries, keys, values, counts, offsets, tree_ids, block_lists):
    any_space = pl.BlockSpec(memory_space=pl.ANY)
    smem = pl.BlockSpec(memory_space=pltpu.SMEM)
    dma = pltpu.SemaphoreType.DMA
    return pl.pallas_call(
        kernel,
        out_shape=jax.ShapeDtypeStruct((TOK_W, KEY_VALUE_HEADS * WIDE), BF16),
        in_specs=[smem] * 4 + [any_space] * 3,
        out_specs=any_space,
        scratch_shapes=[
            pltpu.VMEM((N_HEAD, TOK_W, WIDE), BF16),
            pltpu.VMEM((N_SEQ * ROW, 2 * HEAD_SIZE), BF16),
            pltpu.VMEM((2, N_SEQ, HALF, 2 * HEAD_SIZE), BF16),
            pltpu.VMEM((2, N_SEQ * HALF, HEAD_SIZE), BF16),
            pltpu.VMEM((N_SEQ, N_HEAD, 1, 128), F32),
            pltpu.VMEM((N_SEQ, QB, 1, 128), F32),
            pltpu.VMEM((2, QROWS, 2 * HEAD_SIZE), BF16),
            pltpu.VMEM((2, QROWS, N_SEQ * HALF), F32),
            pltpu.VMEM((2, QROWS, 128), F32),
            pltpu.VMEM((TOK_W, WIDE), BF16),
            pltpu.VMEM((N_HEAD, TOK_W, WIDE), BF16),
            dma((3,)),
            dma((N_HEAD, 2)),
            dma((N_HEAD, 2)),
            dma((N_HEAD,)),
            dma((N_HEAD,)),
            dma((N_HEAD,)),
            dma((N_HEAD,)),
            dma((2, 4, 4)),
            dma((2, 4, 4)),
            dma((N_SEQ,)),
            dma((N_SEQ,)),
            dma((N_SEQ,)),
            dma((N_SEQ,)),
            dma((N_HEAD + 1,)),
            dma((N_HEAD + 1,)),
        ],
        compiler_params=pltpu.CompilerParams(
            collective_id=0, has_side_effects=True, vmem_limit_bytes=62 * 1024 * 1024
        ),
    )(counts, offsets, tree_ids, jnp.transpose(block_lists, (2, 0, 1)), queries, keys, values)


def solution(mesh):
    split = P(("rep", "seq", "head"), None)
    placed = (split,) * 6 + (P(("rep", "seq"), None, None),)
    return jax.shard_map(body, mesh=mesh, in_specs=placed, out_specs=split, check_vma=False)
```

```python
import functools
import math

import jax
import jax.numpy as jnp
from jax import lax
from jax.experimental import pallas as pl
from jax.experimental.pallas import tpu as pltpu
from jax.sharding import PartitionSpec as P

MESH = pl.DeviceIdType.MESH
KEY_VALUE_HEADS = 8
GROUP = 8
HEAD_SIZE = 128
TOK_W = 64
SLOT = 32
ANCESTOR_COUNT = 7
QB = 16
N_SEQ = 8
N_HEAD = 8
ROW = N_HEAD * TOK_W
HALF = ROW // 2
WIDE = GROUP * HEAD_SIZE
TILE = GROUP * SLOT
QROWS = N_HEAD * TILE
FOUR = 4 * TOK_W
PIECE = 2 * TOK_W
ORDER = (0, 1, 3, 2)
NEG = -1e30
FACTOR = math.log2(math.e) / math.sqrt(HEAD_SIZE)
NT = (((1,), (1,)), ((), ()))
BF16 = jnp.bfloat16
F32 = jnp.float32


def kernel(
    cnt_ref, off_ref, tree_ref, bl_ref, q_ref, k_ref, v_ref, out_ref,
    qbuf, kv, ks, vs, moves, turns, ids, anc, qa, sbuf, mx, osort, stage,
    own_sem, kv_s, kv_r, id_s, id_r, q_s, q_r, ring_s, ring_r, idr_s, idr_r, an_s, an_r, o_s, o_r,
):
    z = lax.axis_index("seq")
    h = lax.axis_index("head")
    up = lax.rem(z + 1, N_SEQ)
    down = lax.rem(z + N_SEQ - 1, N_SEQ)

    barrier = pltpu.get_barrier_semaphore()
    for d in range(1, N_HEAD):
        pl.semaphore_signal(barrier, inc=1, device_id={"head": lax.rem(h + d, N_HEAD)}, device_id_type=MESH)
    for d in range(1, N_SEQ):
        pl.semaphore_signal(barrier, inc=1, device_id={"seq": lax.rem(z + d, N_SEQ)}, device_id_type=MESH)

    def cols(p):
        return pl.ds(pl.multiple_of(p * HEAD_SIZE, HEAD_SIZE), HEAD_SIZE)

    def wide(p):
        return pl.ds(pl.multiple_of(p * WIDE, WIDE), WIDE)

    mine = pl.ds(pl.multiple_of(z * ROW + h * TOK_W, TOK_W), TOK_W)
    left, right = pl.ds(0, HEAD_SIZE), pl.ds(HEAD_SIZE, HEAD_SIZE)
    own = [
        pltpu.make_async_copy(k_ref.at[:, cols(h)], kv.at[mine, left], own_sem.at[0]),
        pltpu.make_async_copy(v_ref.at[:, cols(h)], kv.at[mine, right], own_sem.at[1]),
        pltpu.make_async_copy(q_ref.at[:, wide(h)], qbuf.at[h], own_sem.at[2]),
    ]
    for c in own:
        c.start()

    lane1 = lax.broadcasted_iota(jnp.int32, (1, 128), 1)
    info = jnp.zeros((1, 128), F32)
    for s in range(N_SEQ):
        start, count = off_ref[0, s], cnt_ref[0, s]
        member = (lane1 >= start) & (lane1 < start + count)
        info = jnp.where(member, (s * 4 + tree_ref[0, s]).astype(F32), info)
        info = jnp.where(lane1 == TOK_W + s, count.astype(F32), info)
        info = jnp.where(lane1 == TOK_W + N_SEQ + s, start.astype(F32), info)
    ids[z, h] = info
    lane_block = (lane1 - 32) >> 2
    for b in range(QB):
        hit = jnp.zeros((1, 128), F32)
        for k in range(ANCESTOR_COUNT):
            e = bl_ref[k, 0, b]
            hit = jnp.where((lane_block == e) & (lane1 >= 32), 1.0, hit)
        anc[z, b] = hit

    pl.semaphore_wait(barrier, N_HEAD + N_SEQ - 2)

    def remote(src, dst, s_sem, r_sem, **where):
        return pltpu.make_async_remote_copy(
            src_ref=src, dst_ref=dst, send_sem=s_sem, recv_sem=r_sem, device_id=where, device_id_type=MESH
        )

    others = [lax.rem(h + d, N_HEAD) for d in range(N_HEAD)]
    id_row = [remote(ids.at[z, h], ids.at[z, h], id_s.at[d], id_r.at[d], head=others[d]) for d in range(1, N_HEAD)]
    k_row = [
        remote(k_ref.at[:, cols(others[d])], kv.at[mine, left], kv_s.at[d, 0], kv_r.at[d, 0], head=others[d])
        for d in range(1, N_HEAD)
    ]
    v_row = [
        remote(v_ref.at[:, cols(others[d])], kv.at[mine, right], kv_s.at[d, 1], kv_r.at[d, 1], head=others[d])
        for d in range(1, N_HEAD)
    ]
    q_row = [
        remote(q_ref.at[:, wide(others[d])], qbuf.at[h], q_s.at[d], q_r.at[d], head=others[d])
        for d in range(1, N_HEAD)
    ]
    for c in id_row:
        c.start()
    for a, b in zip(k_row, v_row):
        a.start()
        b.start()

    chip = h // 2

    def piece(r, j):
        c = lax.rem(chip + ORDER[j], 4)
        return kv.at[pl.ds(pl.multiple_of(r * ROW + c * PIECE, PIECE), PIECE)]

    def source(way, t):
        return lax.rem(z + N_SEQ - t, N_SEQ) if way == 0 else lax.rem(z + t, N_SEQ)

    def hop(way, t, j):
        ref = piece(source(way, t), j)
        return remote(ref, ref, ring_s.at[way, t, j], ring_r.at[way, t, j], seq=up if way == 0 else down)

    def pieces(way, t):
        return range(4) if t < 3 else (range(2) if way == 0 else range(2, 4))

    ring = {(way, t, j): hop(way, t, j) for way in range(2) for t in range(4) for j in pieces(way, t)}

    def landed(j):
        for q in range(2):
            src = lax.rem(chip + ORDER[j], 4) * 2 + q
            d = lax.rem(h + N_HEAD - src, N_HEAD)

            @pl.when(d == 0)
            def _():
                own[0].wait()
                own[1].wait()

            @pl.when(d != 0)
            def _():
                remote(kv.at[mine, left], kv.at[mine, left], kv_s.at[d, 0], kv_r.at[d, 0], head=src).wait_recv()
                remote(kv.at[mine, right], kv.at[mine, right], kv_s.at[d, 1], kv_r.at[d, 1], head=src).wait_recv()

    for j in range(4):
        landed(j)
        for way in range(2):
            ring[way, 0, j].start()
    for c in q_row:
        c.start()
    for c in id_row:
        c.wait_recv()
    id_col, an_col = [], []
    for e in range(1, N_SEQ):
        to = lax.rem(z + e, N_SEQ)
        id_col.append(remote(ids.at[z], ids.at[z], idr_s.at[e], idr_r.at[e], seq=to))
        two = pl.ds(2 * to, 2)
        an_col.append(remote(anc.at[z, two], anc.at[z, two], an_s.at[e], an_r.at[e], seq=to))
    for c in id_col + an_col:
        c.start()

    def forward(t, j):
        for way in range(2):
            if (way, t - 1, j) in ring:
                ring[way, t - 1, j].wait_recv()
            if (way, t, j) in ring:
                ring[way, t, j].start()

    forward(1, 0)
    forward(1, 1)
    for c in id_col + an_col:
        c.wait_recv()
    least = jnp.full((1, 128), 1e9, F32)
    for r in range(N_SEQ):
        for w in range(N_HEAD):
            least = jnp.minimum(least, ids[r, w])
    lane1f = lane1.astype(F32)
    is_full = (lane1 >= TOK_W) & (lane1 < TOK_W + N_SEQ) & (least > SLOT - 0.5)
    full = jnp.min(jnp.where(is_full, lane1f, 1e9), axis=1, keepdims=True)

    def first_row(r, w):
        return jnp.sum(jnp.where(lane1f == full + N_SEQ, ids[r, w], 0.0), axis=1, keepdims=True)

    lane = lax.broadcasted_iota(jnp.int32, (TOK_W, 128), 1)
    tok = lax.broadcasted_iota(jnp.int32, (TOK_W, 128), 0)

    def column(row):
        return jnp.sum(jnp.where(lane == tok, row, 0.0), axis=1, keepdims=True)

    r4 = lax.broadcasted_iota(jnp.int32, (FOUR, 1), 0)
    c4 = lax.broadcasted_iota(jnp.int32, (FOUR, FOUR), 1).astype(F32)
    who4, place4 = (r4 >> 5) & 3, ((r4 >> 7) * SLOT + (r4 & (SLOT - 1))).astype(F32)

    def mark_keys(r):
        for u in range(2):
            first = jnp.zeros((FOUR, 1), F32)
            parts = []
            for n in range(4):
                w = 4 * u + n
                first = jnp.where(who4 == n, first_row(r, w), first)
                hot = (lane.astype(F32) == column(ids[r, w])) | (lane == 32 + r * N_HEAD + w)
                parts.append(jnp.where(hot, 1.0, 0.0).astype(BF16))
            t = first + place4
            t = jnp.where(t >= TOK_W, t - TOK_W, t) + (who4 * TOK_W).astype(F32)
            move = jnp.where(c4 == t, 1.0, 0.0).astype(BF16)
            moves[r, u] = move
            marks = jnp.dot(move, jnp.concatenate(parts, axis=0), preferred_element_type=F32).astype(BF16)
            for f in range(2):
                ks[f, r, u * 128 : (u + 1) * 128, HEAD_SIZE:] = marks[f * 128 : (f + 1) * 128]

    def sort_keys(r):
        for u in range(2):
            rows = pl.ds(pl.multiple_of(r * ROW + u * FOUR, FOUR), FOUR)
            both = jnp.dot(moves[r, u], kv[rows, :], preferred_element_type=F32).astype(BF16)
            for f in range(2):
                part = slice(f * 128, (f + 1) * 128)
                ks[f, r, u * 128 : (u + 1) * 128, 0:HEAD_SIZE] = both[part, 0:HEAD_SIZE]
                vs[f, pl.ds(pl.multiple_of(r * HALF + u * 128, 128), 128), :] = both[part, HEAD_SIZE:]

    c1 = lax.broadcasted_iota(jnp.int32, (TOK_W, TOK_W), 1).astype(F32)
    r1 = lax.broadcasted_iota(jnp.int32, (TOK_W, TOK_W), 0).astype(F32)

    def mark_queries(p, carry):
        w = z * N_HEAD + p
        b = w // 4
        c = column(ids[z, p])
        shard = jnp.floor(c * 0.25)
        looks = jnp.zeros((TOK_W, 128), F32)
        for s in range(N_SEQ):
            looks = jnp.where(shard == float(s), anc[s, b], looks)
        worker = lane - 32
        own_block = ((worker >> 2) == b) & (worker <= w)
        fine = jnp.where(
            lane < 32,
            jnp.where(lane.astype(F32) == c, 1.0, 0.0),
            jnp.where((lane >= 96) | own_block, 1.0, looks),
        )
        penalty = jnp.where(fine > 0.5, 0.0, NEG).astype(BF16)
        t = first_row(z, p) + r1
        t = jnp.where(t >= TOK_W, t - TOK_W, t)
        move = jnp.where(c1 == t, 1.0, 0.0).astype(BF16)
        turns[p] = move
        marks = jnp.dot(move, penalty, preferred_element_type=F32).astype(BF16)
        for f in range(2):
            part = slice(f * SLOT, (f + 1) * SLOT)
            for g in range(GROUP):
                to = pl.ds(pl.multiple_of(p * TILE + g * SLOT, SLOT), SLOT)
                qa[f, to, HEAD_SIZE:] = marks[part]
        return carry

    def sort_queries(p, carry):
        rows = jnp.dot(turns[p], qbuf[p], preferred_element_type=F32).astype(BF16)
        for f in range(2):
            part = slice(f * SLOT, (f + 1) * SLOT)
            for g in range(GROUP):
                to = pl.ds(pl.multiple_of(p * TILE + g * SLOT, SLOT), SLOT)
                qa[f, to, 0:HEAD_SIZE] = rows[part, g * HEAD_SIZE : (g + 1) * HEAD_SIZE]
        return carry

    BLOCK = 2048
    row_id = lax.broadcasted_iota(jnp.int32, (BLOCK, HALF), 0)
    col_id = lax.broadcasted_iota(jnp.int32, (BLOCK, HALF), 1)
    late_pos = (col_id & (SLOT - 1)) > (row_id & (SLOT - 1))

    def score(r, f, is_own):
        def block(n, carry):
            at = pl.ds(pl.multiple_of(n * BLOCK, BLOCK), BLOCK)
            s = lax.dot_general(qa[f, at, :], ks[f, r], NT, preferred_element_type=F32) * FACTOR
            if is_own:
                late = late_pos & ((col_id >> 5) == (row_id >> 8) + n * (BLOCK // TILE))
                s = jnp.where(late, NEG, s)
            sbuf[f, at, pl.ds(pl.multiple_of(r * HALF, HALF), HALF)] = s
            top = jnp.maximum(s[:, 0:128], s[:, 128:])
            mx[f, at, :] = top if is_own else jnp.maximum(mx[f, at, :], top)
            return carry

        lax.fori_loop(0, QROWS // BLOCK, block, 0)

    def sort_if(r):
        @pl.when(r < bound)
        def _():
            sort_keys(r)

    def score_if(r):
        @pl.when(r < bound)
        def _():
            for f in range(2):
                score(r, f, False)

    def ready_queries():
        own[2].wait()
        for c in q_row:
            c.wait_recv()
        lax.fori_loop(0, N_HEAD, sort_queries, 0)

    bound = jnp.where(z < N_SEQ // 2, N_SEQ // 2, N_SEQ)
    near = {(way, t): source(way, t) for way in range(2) for t in range(1, 4)}
    opposite = lax.rem(z + 4, N_SEQ)
    def mark_if(r):
        @pl.when(r < bound)
        def _():
            mark_keys(r)

    forward(1, 2)
    forward(1, 3)
    mark_keys(z)
    sort_keys(z)
    forward(2, 0)
    forward(2, 1)
    mark_if(near[0, 1])
    mark_if(near[1, 1])
    forward(2, 2)
    forward(2, 3)
    sort_if(near[0, 1])
    sort_if(near[1, 1])
    lax.fori_loop(0, N_HEAD, mark_queries, 0)
    mark_if(near[0, 2])
    forward(3, 0)
    forward(3, 1)
    mark_if(near[1, 2])
    mark_if(near[0, 3])
    forward(3, 2)
    forward(3, 3)
    mark_if(near[1, 3])
    mark_if(opposite)
    sort_if(near[0, 2])
    sort_if(near[1, 2])
    ready_queries()
    score(z, 0, True)
    score(z, 1, True)
    for way in range(2):
        score_if(near[way, 1])
        score_if(near[way, 2])
    for way in range(2):
        sort_if(near[way, 3])
        score_if(near[way, 3])
    for j in range(4):
        forward(4, j)
    sort_if(opposite)
    score_if(opposite)

    def tile(limit, step, carry):
        m = lax.rem(step, 3)
        across = jnp.where(step < 6, 2 - m + 3 * (m // 2), 0)
        other = jnp.where(step < 6, step // 3, 7 - step)
        p = lax.rem(h // 2 + across, 4) * 2 + lax.rem(h + other, 2)
        d = lax.rem(p - h + N_HEAD, N_HEAD)
        at = pl.ds(pl.multiple_of(p * TILE, TILE), TILE)
        keys = limit * HALF
        for f in range(2):
            top = jnp.broadcast_to(jnp.max(mx[f, at, :], axis=1, keepdims=True), (TILE, 128))
            weights = jnp.exp2(sbuf[f, at, 0:keys] - jnp.concatenate([top] * (keys // 128), axis=1))
            total = weights[:, 0:128]
            for n in range(1, keys // 128):
                total = total + weights[:, n * 128 : (n + 1) * 128]
            blend = jnp.dot(weights.astype(BF16), vs[f, 0:keys, :], preferred_element_type=F32)
            done = (blend / jnp.sum(total, axis=1, keepdims=True)).astype(BF16)
            for g in range(GROUP):
                osort[f * SLOT : (f + 1) * SLOT, g * HEAD_SIZE : (g + 1) * HEAD_SIZE] = done[
                    g * SLOT : (g + 1) * SLOT
                ]
        t = r1 - first_row(z, p)
        t = jnp.where(t < 0.0, t + TOK_W, t)
        back = jnp.where(c1 == t, 1.0, 0.0).astype(BF16)
        stage[p] = jnp.dot(back, osort[...], preferred_element_type=F32).astype(BF16)

        @pl.when(p != h)
        def _():
            remote(stage.at[p], out_ref.at[:, wide(h)], o_s.at[d], o_r.at[d], head=p).start()

        return carry

    for limit in (N_SEQ // 2, N_SEQ):

        @pl.when(bound == limit)
        def _():
            lax.fori_loop(0, N_HEAD, functools.partial(tile, limit), 0)

    last = pltpu.make_async_copy(stage.at[h], out_ref.at[:, wide(h)], own_sem.at[0])
    last.start()
    last.wait()
    for c in id_row + k_row + v_row + q_row + id_col + an_col + list(ring.values()):
        c.wait_send()
    for d in range(1, N_HEAD):
        p = lax.rem(h + d, N_HEAD)
        remote(stage.at[p], out_ref.at[:, wide(h)], o_s.at[d], o_r.at[d], head=p).wait()


def body(queries, keys, values, counts, offsets, tree_ids, block_lists):
    any_space = pl.BlockSpec(memory_space=pl.ANY)
    smem = pl.BlockSpec(memory_space=pltpu.SMEM)
    dma = pltpu.SemaphoreType.DMA
    return pl.pallas_call(
        kernel,
        out_shape=jax.ShapeDtypeStruct((TOK_W, KEY_VALUE_HEADS * WIDE), BF16),
        in_specs=[smem] * 4 + [pl.BlockSpec(memory_space=pltpu.HBM)] * 3,
        out_specs=any_space,
        scratch_shapes=[
            pltpu.VMEM((N_HEAD, TOK_W, WIDE), BF16),
            pltpu.VMEM((N_SEQ * ROW, 2 * HEAD_SIZE), BF16),
            pltpu.VMEM((2, N_SEQ, HALF, 2 * HEAD_SIZE), BF16),
            pltpu.VMEM((2, N_SEQ * HALF, HEAD_SIZE), BF16),
            pltpu.VMEM((N_SEQ, 2, FOUR, FOUR), BF16),
            pltpu.VMEM((N_HEAD, TOK_W, TOK_W), BF16),
            pltpu.VMEM((N_SEQ, N_HEAD, 1, 128), F32),
            pltpu.VMEM((N_SEQ, QB, 1, 128), F32),
            pltpu.VMEM((2, QROWS, 2 * HEAD_SIZE), BF16),
            pltpu.VMEM((2, QROWS, N_SEQ * HALF), F32),
            pltpu.VMEM((2, QROWS, 128), F32),
            pltpu.VMEM((TOK_W, WIDE), BF16),
            pltpu.VMEM((N_HEAD, TOK_W, WIDE), BF16),
            dma((3,)),
            dma((N_HEAD, 2)),
            dma((N_HEAD, 2)),
            dma((N_HEAD,)),
            dma((N_HEAD,)),
            dma((N_HEAD,)),
            dma((N_HEAD,)),
            dma((2, 4, 4)),
            dma((2, 4, 4)),
            dma((N_SEQ,)),
            dma((N_SEQ,)),
            dma((N_SEQ,)),
            dma((N_SEQ,)),
            dma((N_HEAD + 1,)),
            dma((N_HEAD + 1,)),
        ],
        compiler_params=pltpu.CompilerParams(
            collective_id=0, has_side_effects=True, vmem_limit_bytes=58 * 1024 * 1024
        ),
    )(counts, offsets, tree_ids, jnp.transpose(block_lists, (2, 0, 1)), queries, keys, values)


def solution(mesh):
    split = P(("rep", "seq", "head"), None)
    placed = (split,) * 6 + (P(("rep", "seq"), None, None),)
    return jax.shard_map(body, mesh=mesh, in_specs=placed, out_specs=split, check_vma=False)
```

```python
import functools
import math

import jax
import jax.numpy as jnp
from jax import lax
from jax.experimental import pallas as pl
from jax.experimental.pallas import tpu as pltpu
from jax.sharding import PartitionSpec as P

MESH = pl.DeviceIdType.MESH
KEY_VALUE_HEADS = 8
GROUP = 8
HEAD_SIZE = 128
TOK_W = 64
SLOT = 32
ANCESTOR_COUNT = 7
QB = 16
N_SEQ = 8
N_HEAD = 8
ROW = N_HEAD * TOK_W
HALF = ROW // 2
WIDE = GROUP * HEAD_SIZE
TILE = GROUP * SLOT
QROWS = N_HEAD * TILE
FOUR = 4 * TOK_W
PIECE = 2 * TOK_W
ORDER = (0, 1, 3, 2)
NEG = -1e30
FACTOR = math.log2(math.e) / math.sqrt(HEAD_SIZE)
NT = (((1,), (1,)), ((), ()))
BF16 = jnp.bfloat16
F32 = jnp.float32


def kernel(
    cnt_ref, off_ref, tree_ref, bl_ref, q_ref, k_ref, v_ref, out_ref,
    qbuf, kv, ks, vs, moves, turns, ids, anc, qa, sbuf, mx, osort, stage,
    own_sem, kv_s, kv_r, id_s, id_r, q_s, q_r, ring_s, ring_r, idr_s, idr_r, an_s, an_r, o_s, o_r,
):
    z = lax.axis_index("seq")
    h = lax.axis_index("head")
    up = lax.rem(z + 1, N_SEQ)
    down = lax.rem(z + N_SEQ - 1, N_SEQ)

    barrier = pltpu.get_barrier_semaphore()
    for d in range(1, N_HEAD):
        pl.semaphore_signal(barrier, inc=1, device_id={"head": lax.rem(h + d, N_HEAD)}, device_id_type=MESH)
    for d in range(1, N_SEQ):
        pl.semaphore_signal(barrier, inc=1, device_id={"seq": lax.rem(z + d, N_SEQ)}, device_id_type=MESH)

    def cols(p):
        return pl.ds(pl.multiple_of(p * HEAD_SIZE, HEAD_SIZE), HEAD_SIZE)

    def wide(p):
        return pl.ds(pl.multiple_of(p * WIDE, WIDE), WIDE)

    mine = pl.ds(pl.multiple_of(z * ROW + h * TOK_W, TOK_W), TOK_W)
    left, right = pl.ds(0, HEAD_SIZE), pl.ds(HEAD_SIZE, HEAD_SIZE)
    own = [
        pltpu.make_async_copy(k_ref.at[:, cols(h)], kv.at[mine, left], own_sem.at[0]),
        pltpu.make_async_copy(v_ref.at[:, cols(h)], kv.at[mine, right], own_sem.at[1]),
        pltpu.make_async_copy(q_ref.at[:, wide(h)], qbuf.at[h], own_sem.at[2]),
    ]
    for c in own:
        c.start()

    lane1 = lax.broadcasted_iota(jnp.int32, (1, 128), 1)
    info = jnp.zeros((1, 128), F32)
    for s in range(N_SEQ):
        start, count = off_ref[0, s], cnt_ref[0, s]
        member = (lane1 >= start) & (lane1 < start + count)
        info = jnp.where(member, (s * 4 + tree_ref[0, s]).astype(F32), info)
        info = jnp.where(lane1 == TOK_W + s, count.astype(F32), info)
        info = jnp.where(lane1 == TOK_W + N_SEQ + s, start.astype(F32), info)
    ids[z, h] = info
    lane_block = (lane1 - 32) >> 2
    for b in range(QB):
        hit = jnp.zeros((1, 128), F32)
        for k in range(ANCESTOR_COUNT):
            e = bl_ref[k, 0, b]
            hit = jnp.where((lane_block == e) & (lane1 >= 32), 1.0, hit)
        anc[z, b] = hit

    pl.semaphore_wait(barrier, N_HEAD + N_SEQ - 2)

    def remote(src, dst, s_sem, r_sem, **where):
        return pltpu.make_async_remote_copy(
            src_ref=src, dst_ref=dst, send_sem=s_sem, recv_sem=r_sem, device_id=where, device_id_type=MESH
        )

    core = lax.rem(h, 2)
    others = [
        lax.rem(h // 2 + across, 4) * 2 + lax.rem(core + other, 2)
        for across, other in ((0, 1), (1, 0), (3, 0), (1, 1), (3, 1), (2, 0), (2, 1))
    ]
    apart = [lax.rem(p - h + N_HEAD, N_HEAD) for p in others]
    id_row = [remote(ids.at[z, h], ids.at[z, h], id_s.at[d], id_r.at[d], head=p) for p, d in zip(others, apart)]
    k_row = [
        remote(k_ref.at[:, cols(p)], kv.at[mine, left], kv_s.at[d, 0], kv_r.at[d, 0], head=p)
        for p, d in zip(others, apart)
    ]
    v_row = [
        remote(v_ref.at[:, cols(p)], kv.at[mine, right], kv_s.at[d, 1], kv_r.at[d, 1], head=p)
        for p, d in zip(others, apart)
    ]
    q_row = [
        remote(q_ref.at[:, wide(p)], qbuf.at[h], q_s.at[d], q_r.at[d], head=p)
        for p, d in zip(others, apart)
    ]
    for a, b in zip(k_row, v_row):
        a.start()
        b.start()
    for c in id_row:
        c.start()

    chip = h // 2

    def piece(r, j):
        c = lax.rem(chip + ORDER[j], 4)
        return kv.at[pl.ds(pl.multiple_of(r * ROW + c * PIECE, PIECE), PIECE)]

    def source(way, t):
        return lax.rem(z + N_SEQ - t, N_SEQ) if way == 0 else lax.rem(z + t, N_SEQ)

    def hop(way, t, j):
        ref = piece(source(way, t), j)
        return remote(ref, ref, ring_s.at[way, t, j], ring_r.at[way, t, j], seq=up if way == 0 else down)

    def pieces(way, t):
        return range(4) if t < 3 else (range(2) if way == 0 else range(2, 4))

    ring = {(way, t, j): hop(way, t, j) for way in range(2) for t in range(4) for j in pieces(way, t)}

    def landed(j):
        for q in range(2):
            src = lax.rem(chip + ORDER[j], 4) * 2 + q
            d = lax.rem(h + N_HEAD - src, N_HEAD)

            @pl.when(d == 0)
            def _():
                own[0].wait()
                own[1].wait()

            @pl.when(d != 0)
            def _():
                remote(kv.at[mine, left], kv.at[mine, left], kv_s.at[d, 0], kv_r.at[d, 0], head=src).wait_recv()
                remote(kv.at[mine, right], kv.at[mine, right], kv_s.at[d, 1], kv_r.at[d, 1], head=src).wait_recv()

    for j in range(4):
        landed(j)
        for way in range(2):
            ring[way, 0, j].start()
    for c in q_row:
        c.start()
    for c in id_row:
        c.wait_recv()
    id_col, an_col = [], []
    for e in range(1, N_SEQ):
        to = lax.rem(z + e, N_SEQ)
        id_col.append(remote(ids.at[z], ids.at[z], idr_s.at[e], idr_r.at[e], seq=to))
        two = pl.ds(2 * to, 2)
        an_col.append(remote(anc.at[z, two], anc.at[z, two], an_s.at[e], an_r.at[e], seq=to))
    for c in id_col + an_col:
        c.start()

    def forward(t, j):
        for way in range(2):
            if (way, t - 1, j) in ring:
                ring[way, t - 1, j].wait_recv()
            if (way, t, j) in ring:
                ring[way, t, j].start()

    forward(1, 0)
    forward(1, 1)
    for c in id_col + an_col:
        c.wait_recv()
    least = jnp.full((1, 128), 1e9, F32)
    for r in range(N_SEQ):
        for w in range(N_HEAD):
            least = jnp.minimum(least, ids[r, w])
    lane1f = lane1.astype(F32)
    is_full = (lane1 >= TOK_W) & (lane1 < TOK_W + N_SEQ) & (least > SLOT - 0.5)
    full = jnp.min(jnp.where(is_full, lane1f, 1e9), axis=1, keepdims=True)

    def first_row(r, w):
        return jnp.sum(jnp.where(lane1f == full + N_SEQ, ids[r, w], 0.0), axis=1, keepdims=True)

    lane = lax.broadcasted_iota(jnp.int32, (TOK_W, 128), 1)
    tok = lax.broadcasted_iota(jnp.int32, (TOK_W, 128), 0)

    def column(row):
        return jnp.sum(jnp.where(lane == tok, row, 0.0), axis=1, keepdims=True)

    r4 = lax.broadcasted_iota(jnp.int32, (FOUR, 1), 0)
    c4 = lax.broadcasted_iota(jnp.int32, (FOUR, FOUR), 1).astype(F32)
    who4, place4 = (r4 >> 5) & 3, ((r4 >> 7) * SLOT + (r4 & (SLOT - 1))).astype(F32)

    def mark_keys(r):
        for u in range(2):
            first = jnp.zeros((FOUR, 1), F32)
            parts = []
            for n in range(4):
                w = 4 * u + n
                first = jnp.where(who4 == n, first_row(r, w), first)
                hot = (lane.astype(F32) == column(ids[r, w])) | (lane == 32 + r * N_HEAD + w)
                parts.append(jnp.where(hot, 1.0, 0.0).astype(BF16))
            t = first + place4
            t = jnp.where(t >= TOK_W, t - TOK_W, t) + (who4 * TOK_W).astype(F32)
            move = jnp.where(c4 == t, 1.0, 0.0).astype(BF16)
            moves[r, u] = move
            marks = jnp.dot(move, jnp.concatenate(parts, axis=0), preferred_element_type=F32).astype(BF16)
            for f in range(2):
                ks[f, r, u * 128 : (u + 1) * 128, HEAD_SIZE:] = marks[f * 128 : (f + 1) * 128]

    def sort_keys(r):
        for u in range(2):
            rows = pl.ds(pl.multiple_of(r * ROW + u * FOUR, FOUR), FOUR)
            both = jnp.dot(moves[r, u], kv[rows, :], preferred_element_type=F32).astype(BF16)
            for f in range(2):
                part = slice(f * 128, (f + 1) * 128)
                ks[f, r, u * 128 : (u + 1) * 128, 0:HEAD_SIZE] = both[part, 0:HEAD_SIZE]
                vs[f, pl.ds(pl.multiple_of(r * HALF + u * 128, 128), 128), :] = both[part, HEAD_SIZE:]

    c1 = lax.broadcasted_iota(jnp.int32, (TOK_W, TOK_W), 1).astype(F32)
    r1 = lax.broadcasted_iota(jnp.int32, (TOK_W, TOK_W), 0).astype(F32)

    def mark_queries(p):
        w = z * N_HEAD + p
        b = w // 4
        c = column(ids[z, p])
        shard = jnp.floor(c * 0.25)
        looks = jnp.zeros((TOK_W, 128), F32)
        for s in range(N_SEQ):
            looks = jnp.where(shard == float(s), anc[s, b], looks)
        worker = lane - 32
        own_block = ((worker >> 2) == b) & (worker <= w)
        fine = jnp.where(
            lane < 32,
            jnp.where(lane.astype(F32) == c, 1.0, 0.0),
            jnp.where((lane >= 96) | own_block, 1.0, looks),
        )
        penalty = jnp.where(fine > 0.5, 0.0, NEG).astype(BF16)
        t = first_row(z, p) + r1
        t = jnp.where(t >= TOK_W, t - TOK_W, t)
        move = jnp.where(c1 == t, 1.0, 0.0).astype(BF16)
        turns[p] = move
        marks = jnp.dot(move, penalty, preferred_element_type=F32).astype(BF16)
        for f in range(2):
            part = slice(f * SLOT, (f + 1) * SLOT)
            for g in range(GROUP):
                to = pl.ds(p * TILE + g * SLOT, SLOT)
                qa[f, to, HEAD_SIZE:] = marks[part]

    def sort_queries(p):
        rows = jnp.dot(turns[p], qbuf[p], preferred_element_type=F32).astype(BF16)
        for f in range(2):
            part = slice(f * SLOT, (f + 1) * SLOT)
            for g in range(GROUP):
                to = pl.ds(p * TILE + g * SLOT, SLOT)
                qa[f, to, 0:HEAD_SIZE] = rows[part, g * HEAD_SIZE : (g + 1) * HEAD_SIZE]

    BLOCK = 2048
    row_id = lax.broadcasted_iota(jnp.int32, (BLOCK, HALF), 0)
    col_id = lax.broadcasted_iota(jnp.int32, (BLOCK, HALF), 1)
    late_pos = (col_id & (SLOT - 1)) > (row_id & (SLOT - 1))

    def score(r, f, is_own):
        def block(n, carry):
            at = pl.ds(pl.multiple_of(n * BLOCK, BLOCK), BLOCK)
            s = lax.dot_general(qa[f, at, :], ks[f, r], NT, preferred_element_type=F32) * FACTOR
            if is_own:
                late = late_pos & ((col_id >> 5) == (row_id >> 8) + n * (BLOCK // TILE))
                s = jnp.where(late, NEG, s)
            sbuf[f, at, pl.ds(pl.multiple_of(r * HALF, HALF), HALF)] = s
            top = jnp.maximum(s[:, 0:128], s[:, 128:])
            mx[f, at, :] = top if is_own else jnp.maximum(mx[f, at, :], top)
            return carry

        lax.fori_loop(0, QROWS // BLOCK, block, 0)

    def sort_if(r):
        @pl.when(r < bound)
        def _():
            sort_keys(r)

    def score_if(r):
        @pl.when(r < bound)
        def _():
            for f in range(2):
                score(r, f, False)

    def ready_queries():
        own[2].wait()
        for c in q_row:
            c.wait_recv()
        for p in range(N_HEAD):
            sort_queries(p)

    bound = jnp.where(z < N_SEQ // 2, N_SEQ // 2, N_SEQ)
    near = {(way, t): source(way, t) for way in range(2) for t in range(1, 4)}
    opposite = lax.rem(z + 4, N_SEQ)
    def mark_if(r):
        @pl.when(r < bound)
        def _():
            mark_keys(r)

    forward(1, 2)
    mark_keys(z)
    forward(1, 3)
    mark_if(near[0, 1])
    forward(2, 0)
    mark_if(near[1, 1])
    forward(2, 1)
    mark_if(near[0, 2])
    forward(2, 2)
    mark_if(near[1, 2])
    forward(2, 3)
    mark_if(near[0, 3])
    for p in range(N_HEAD // 2):
        mark_queries(p)
    forward(3, 0)
    mark_if(near[1, 3])
    for p in range(N_HEAD // 2, N_HEAD):
        mark_queries(p)
    forward(3, 1)
    mark_if(opposite)
    sort_keys(z)
    forward(3, 2)
    sort_if(near[0, 1])
    sort_if(near[1, 1])
    forward(3, 3)
    sort_if(near[0, 2])
    sort_if(near[1, 2])
    ready_queries()
    score(z, 0, True)
    score(z, 1, True)
    for way in range(2):
        score_if(near[way, 1])
        score_if(near[way, 2])
    forward(4, 0)
    forward(4, 2)
    for way in range(2):
        sort_if(near[way, 3])
        score_if(near[way, 3])
    forward(4, 1)
    forward(4, 3)
    sort_if(opposite)
    score_if(opposite)

    def tile(limit, step, carry):
        m = lax.rem(step, 3)
        across = jnp.where(step < 6, 2 - m + 3 * (m // 2), 0)
        other = jnp.where(step < 6, step // 3, 7 - step)
        p = lax.rem(h // 2 + across, 4) * 2 + lax.rem(h + other, 2)
        d = lax.rem(p - h + N_HEAD, N_HEAD)
        at = pl.ds(pl.multiple_of(p * TILE, TILE), TILE)
        keys = limit * HALF
        for f in range(2):
            top = jnp.broadcast_to(jnp.max(mx[f, at, :], axis=1, keepdims=True), (TILE, 128))
            weights = jnp.exp2(sbuf[f, at, 0:keys] - jnp.concatenate([top] * (keys // 128), axis=1))
            total = weights[:, 0:128]
            for n in range(1, keys // 128):
                total = total + weights[:, n * 128 : (n + 1) * 128]
            blend = jnp.dot(weights.astype(BF16), vs[f, 0:keys, :], preferred_element_type=F32)
            done = (blend / jnp.sum(total, axis=1, keepdims=True)).astype(BF16)
            for g in range(GROUP):
                osort[f * SLOT : (f + 1) * SLOT, g * HEAD_SIZE : (g + 1) * HEAD_SIZE] = done[
                    g * SLOT : (g + 1) * SLOT
                ]
        t = r1 - first_row(z, p)
        t = jnp.where(t < 0.0, t + TOK_W, t)
        back = jnp.where(c1 == t, 1.0, 0.0).astype(BF16)
        stage[p] = jnp.dot(back, osort[...], preferred_element_type=F32).astype(BF16)

        @pl.when(p != h)
        def _():
            remote(stage.at[p], out_ref.at[:, wide(h)], o_s.at[d], o_r.at[d], head=p).start()

        return carry

    for limit in (N_SEQ // 2, N_SEQ):

        @pl.when(bound == limit)
        def _():
            lax.fori_loop(0, N_HEAD, functools.partial(tile, limit), 0)

    last = pltpu.make_async_copy(stage.at[h], out_ref.at[:, wide(h)], own_sem.at[0])
    last.start()
    last.wait()
    for c in id_row + k_row + v_row + q_row + id_col + an_col + list(ring.values()):
        c.wait_send()
    for d in range(1, N_HEAD):
        p = lax.rem(h + d, N_HEAD)
        remote(stage.at[p], out_ref.at[:, wide(h)], o_s.at[d], o_r.at[d], head=p).wait()


def body(queries, keys, values, counts, offsets, tree_ids, block_lists):
    any_space = pl.BlockSpec(memory_space=pl.ANY)
    smem = pl.BlockSpec(memory_space=pltpu.SMEM)
    dma = pltpu.SemaphoreType.DMA
    return pl.pallas_call(
        kernel,
        out_shape=jax.ShapeDtypeStruct((TOK_W, KEY_VALUE_HEADS * WIDE), BF16),
        in_specs=[smem] * 4 + [pl.BlockSpec(memory_space=pltpu.HBM)] * 3,
        out_specs=any_space,
        scratch_shapes=[
            pltpu.VMEM((N_HEAD, TOK_W, WIDE), BF16),
            pltpu.VMEM((N_SEQ * ROW, 2 * HEAD_SIZE), BF16),
            pltpu.VMEM((2, N_SEQ, HALF, 2 * HEAD_SIZE), BF16),
            pltpu.VMEM((2, N_SEQ * HALF, HEAD_SIZE), BF16),
            pltpu.VMEM((N_SEQ, 2, FOUR, FOUR), BF16),
            pltpu.VMEM((N_HEAD, TOK_W, TOK_W), BF16),
            pltpu.VMEM((N_SEQ, N_HEAD, 1, 128), F32),
            pltpu.VMEM((N_SEQ, QB, 1, 128), F32),
            pltpu.VMEM((2, QROWS, 2 * HEAD_SIZE), BF16),
            pltpu.VMEM((2, QROWS, N_SEQ * HALF), F32),
            pltpu.VMEM((2, QROWS, 128), F32),
            pltpu.VMEM((TOK_W, WIDE), BF16),
            pltpu.VMEM((N_HEAD, TOK_W, WIDE), BF16),
            dma((3,)),
            dma((N_HEAD, 2)),
            dma((N_HEAD, 2)),
            dma((N_HEAD,)),
            dma((N_HEAD,)),
            dma((N_HEAD,)),
            dma((N_HEAD,)),
            dma((2, 4, 4)),
            dma((2, 4, 4)),
            dma((N_SEQ,)),
            dma((N_SEQ,)),
            dma((N_SEQ,)),
            dma((N_SEQ,)),
            dma((N_HEAD + 1,)),
            dma((N_HEAD + 1,)),
        ],
        compiler_params=pltpu.CompilerParams(
            collective_id=0, has_side_effects=True, vmem_limit_bytes=58 * 1024 * 1024
        ),
    )(counts, offsets, tree_ids, jnp.transpose(block_lists, (2, 0, 1)), queries, keys, values)


def solution(mesh):
    split = P(("rep", "seq", "head"), None)
    placed = (split,) * 6 + (P(("rep", "seq"), None, None),)
    return jax.shard_map(body, mesh=mesh, in_specs=placed, out_specs=split, check_vma=False)
```

```python
import functools
import math

import jax
import jax.numpy as jnp
from jax import lax
from jax.experimental import pallas as pl
from jax.experimental.pallas import tpu as pltpu
from jax.sharding import PartitionSpec as P

MESH = pl.DeviceIdType.MESH
KEY_VALUE_HEADS = 8
GROUP = 8
HEAD_SIZE = 128
TOK_W = 64
SLOT = 32
ANCESTOR_COUNT = 7
QB = 16
N_SEQ = 8
N_HEAD = 8
ROW = N_HEAD * TOK_W
HALF = ROW // 2
WIDE = GROUP * HEAD_SIZE
TILE = GROUP * SLOT
QROWS = N_HEAD * TILE
FOUR = 4 * TOK_W
PIECE = 2 * TOK_W
ORDER = (0, 1, 3, 2)
NEG = -1e30
FACTOR = math.log2(math.e) / math.sqrt(HEAD_SIZE)
NT = (((1,), (1,)), ((), ()))
BF16 = jnp.bfloat16
F32 = jnp.float32


def kernel(
    cnt_ref, off_ref, tree_ref, bl_ref, q_ref, k_ref, v_ref, out_ref,
    qbuf, kv, ks, vs, moves, turns, ids, anc, qa, sbuf, mx, osort, stage,
    own_sem, kv_s, kv_r, id_s, id_r, q_s, q_r, ring_s, ring_r, idr_s, idr_r, an_s, an_r, o_s, o_r,
):
    z = lax.axis_index("seq")
    h = lax.axis_index("head")
    up = lax.rem(z + 1, N_SEQ)
    down = lax.rem(z + N_SEQ - 1, N_SEQ)

    barrier = pltpu.get_barrier_semaphore()
    for d in range(1, N_HEAD):
        pl.semaphore_signal(barrier, inc=1, device_id={"head": lax.rem(h + d, N_HEAD)}, device_id_type=MESH)
    for d in range(1, N_SEQ):
        pl.semaphore_signal(barrier, inc=1, device_id={"seq": lax.rem(z + d, N_SEQ)}, device_id_type=MESH)

    def cols(p):
        return pl.ds(pl.multiple_of(p * HEAD_SIZE, HEAD_SIZE), HEAD_SIZE)

    def wide(p):
        return pl.ds(pl.multiple_of(p * WIDE, WIDE), WIDE)

    mine = pl.ds(pl.multiple_of(z * ROW + h * TOK_W, TOK_W), TOK_W)
    left, right = pl.ds(0, HEAD_SIZE), pl.ds(HEAD_SIZE, HEAD_SIZE)
    own = [
        pltpu.make_async_copy(k_ref.at[:, cols(h)], kv.at[mine, left], own_sem.at[0]),
        pltpu.make_async_copy(v_ref.at[:, cols(h)], kv.at[mine, right], own_sem.at[1]),
        pltpu.make_async_copy(q_ref.at[:, wide(h)], qbuf.at[h], own_sem.at[2]),
    ]
    for c in own:
        c.start()

    lane1 = lax.broadcasted_iota(jnp.int32, (1, 128), 1)
    info = jnp.zeros((1, 128), F32)
    for s in range(N_SEQ):
        start, count = off_ref[0, s], cnt_ref[0, s]
        member = (lane1 >= start) & (lane1 < start + count)
        info = jnp.where(member, (s * 4 + tree_ref[0, s]).astype(F32), info)
        info = jnp.where(lane1 == TOK_W + s, count.astype(F32), info)
        info = jnp.where(lane1 == TOK_W + N_SEQ + s, start.astype(F32), info)
    ids[z, h] = info
    lane_block = (lane1 - 32) >> 2
    for b in range(QB):
        hit = jnp.zeros((1, 128), F32)
        for k in range(ANCESTOR_COUNT):
            e = bl_ref[k, 0, b]
            hit = jnp.where((lane_block == e) & (lane1 >= 32), 1.0, hit)
        anc[z, b] = hit

    pl.semaphore_wait(barrier, N_HEAD + N_SEQ - 2)

    def remote(src, dst, s_sem, r_sem, **where):
        return pltpu.make_async_remote_copy(
            src_ref=src, dst_ref=dst, send_sem=s_sem, recv_sem=r_sem, device_id=where, device_id_type=MESH
        )

    core = lax.rem(h, 2)
    others = [
        lax.rem(h // 2 + across, 4) * 2 + lax.rem(core + other, 2)
        for across, other in ((0, 1), (1, 0), (3, 0), (1, 1), (3, 1), (2, 0), (2, 1))
    ]
    apart = [lax.rem(p - h + N_HEAD, N_HEAD) for p in others]
    id_row = [remote(ids.at[z, h], ids.at[z, h], id_s.at[d], id_r.at[d], head=p) for p, d in zip(others, apart)]
    k_row = [
        remote(k_ref.at[:, cols(p)], kv.at[mine, left], kv_s.at[d, 0], kv_r.at[d, 0], head=p)
        for p, d in zip(others, apart)
    ]
    v_row = [
        remote(v_ref.at[:, cols(p)], kv.at[mine, right], kv_s.at[d, 1], kv_r.at[d, 1], head=p)
        for p, d in zip(others, apart)
    ]
    q_row = [
        remote(q_ref.at[:, wide(p)], qbuf.at[h], q_s.at[d], q_r.at[d], head=p)
        for p, d in zip(others, apart)
    ]
    for a, b in zip(k_row, v_row):
        a.start()
        b.start()
    for c in id_row:
        c.start()

    chip = h // 2

    def piece(r, j):
        c = lax.rem(chip + ORDER[j], 4)
        return kv.at[pl.ds(pl.multiple_of(r * ROW + c * PIECE, PIECE), PIECE)]

    def source(way, t):
        return lax.rem(z + N_SEQ - t, N_SEQ) if way == 0 else lax.rem(z + t, N_SEQ)

    def hop(way, t, j):
        ref = piece(source(way, t), j)
        return remote(ref, ref, ring_s.at[way, t, j], ring_r.at[way, t, j], seq=up if way == 0 else down)

    def pieces(way, t):
        return range(4) if t < 3 else (range(2) if way == 0 else range(2, 4))

    ring = {(way, t, j): hop(way, t, j) for way in range(2) for t in range(4) for j in pieces(way, t)}

    def goes(way, t):
        return (z < N_SEQ - 1) & (z >= t) if way == 0 else source(1, t) < N_SEQ // 2

    def comes(way, t):
        return z > t if way == 0 else lax.rem(z + 1 + t, N_SEQ) < N_SEQ // 2

    def landed(j):
        for q in range(2):
            src = lax.rem(chip + ORDER[j], 4) * 2 + q
            d = lax.rem(h + N_HEAD - src, N_HEAD)

            @pl.when(d == 0)
            def _():
                own[0].wait()
                own[1].wait()

            @pl.when(d != 0)
            def _():
                remote(kv.at[mine, left], kv.at[mine, left], kv_s.at[d, 0], kv_r.at[d, 0], head=src).wait_recv()
                remote(kv.at[mine, right], kv.at[mine, right], kv_s.at[d, 1], kv_r.at[d, 1], head=src).wait_recv()

    for j in range(4):
        landed(j)
        for way in range(2):

            @pl.when(goes(way, 0))
            def _():
                ring[way, 0, j].start()

    for c in q_row:
        c.start()
    for c in id_row:
        c.wait_recv()
    id_col, an_col = [], []
    for e in range(1, N_SEQ):
        to = lax.rem(z + e, N_SEQ)
        id_col.append(remote(ids.at[z], ids.at[z], idr_s.at[e], idr_r.at[e], seq=to))
        two = pl.ds(2 * to, 2)
        an_col.append(remote(anc.at[z, two], anc.at[z, two], an_s.at[e], an_r.at[e], seq=to))
    for c in id_col + an_col:
        c.start()

    def forward(t, j):
        for way in range(2):
            if (way, t - 1, j) in ring:

                @pl.when(comes(way, t - 1))
                def _():
                    ring[way, t - 1, j].wait_recv()

            if (way, t, j) in ring:

                @pl.when(goes(way, t))
                def _():
                    ring[way, t, j].start()


    forward(1, 0)
    forward(1, 1)
    for c in id_col + an_col:
        c.wait_recv()
    least = jnp.full((1, 128), 1e9, F32)
    for r in range(N_SEQ):
        for w in range(N_HEAD):
            least = jnp.minimum(least, ids[r, w])
    lane1f = lane1.astype(F32)
    is_full = (lane1 >= TOK_W) & (lane1 < TOK_W + N_SEQ) & (least > SLOT - 0.5)
    full = jnp.min(jnp.where(is_full, lane1f, 1e9), axis=1, keepdims=True)

    def first_row(r, w):
        return jnp.sum(jnp.where(lane1f == full + N_SEQ, ids[r, w], 0.0), axis=1, keepdims=True)

    lane = lax.broadcasted_iota(jnp.int32, (TOK_W, 128), 1)
    tok = lax.broadcasted_iota(jnp.int32, (TOK_W, 128), 0)

    def column(row):
        return jnp.sum(jnp.where(lane == tok, row, 0.0), axis=1, keepdims=True)

    r4 = lax.broadcasted_iota(jnp.int32, (FOUR, 1), 0)
    c4 = lax.broadcasted_iota(jnp.int32, (FOUR, FOUR), 1).astype(F32)
    who4, place4 = (r4 >> 5) & 3, ((r4 >> 7) * SLOT + (r4 & (SLOT - 1))).astype(F32)

    def mark_keys(r):
        for u in range(2):
            first = jnp.zeros((FOUR, 1), F32)
            parts = []
            for n in range(4):
                w = 4 * u + n
                first = jnp.where(who4 == n, first_row(r, w), first)
                hot = (lane.astype(F32) == column(ids[r, w])) | (lane == 32 + r * N_HEAD + w)
                parts.append(jnp.where(hot, 1.0, 0.0).astype(BF16))
            t = first + place4
            t = jnp.where(t >= TOK_W, t - TOK_W, t) + (who4 * TOK_W).astype(F32)
            move = jnp.where(c4 == t, 1.0, 0.0).astype(BF16)
            moves[r, u] = move
            marks = jnp.dot(move, jnp.concatenate(parts, axis=0), preferred_element_type=F32).astype(BF16)
            for f in range(2):
                ks[f, r, u * 128 : (u + 1) * 128, HEAD_SIZE:] = marks[f * 128 : (f + 1) * 128]

    def sort_keys(r):
        for u in range(2):
            rows = pl.ds(pl.multiple_of(r * ROW + u * FOUR, FOUR), FOUR)
            both = jnp.dot(moves[r, u], kv[rows, :], preferred_element_type=F32).astype(BF16)
            for f in range(2):
                part = slice(f * 128, (f + 1) * 128)
                ks[f, r, u * 128 : (u + 1) * 128, 0:HEAD_SIZE] = both[part, 0:HEAD_SIZE]
                vs[f, pl.ds(pl.multiple_of(r * HALF + u * 128, 128), 128), :] = both[part, HEAD_SIZE:]

    c1 = lax.broadcasted_iota(jnp.int32, (TOK_W, TOK_W), 1).astype(F32)
    r1 = lax.broadcasted_iota(jnp.int32, (TOK_W, TOK_W), 0).astype(F32)

    def mark_queries(p):
        w = z * N_HEAD + p
        b = w // 4
        c = column(ids[z, p])
        shard = jnp.floor(c * 0.25)
        looks = jnp.zeros((TOK_W, 128), F32)
        for s in range(N_SEQ):
            looks = jnp.where(shard == float(s), anc[s, b], looks)
        worker = lane - 32
        own_block = ((worker >> 2) == b) & (worker <= w)
        fine = jnp.where(
            lane < 32,
            jnp.where(lane.astype(F32) == c, 1.0, 0.0),
            jnp.where((lane >= 96) | own_block, 1.0, looks),
        )
        penalty = jnp.where(fine > 0.5, 0.0, NEG).astype(BF16)
        t = first_row(z, p) + r1
        t = jnp.where(t >= TOK_W, t - TOK_W, t)
        move = jnp.where(c1 == t, 1.0, 0.0).astype(BF16)
        turns[p] = move
        marks = jnp.dot(move, penalty, preferred_element_type=F32).astype(BF16)
        for f in range(2):
            part = slice(f * SLOT, (f + 1) * SLOT)
            for g in range(GROUP):
                to = pl.ds(p * TILE + g * SLOT, SLOT)
                qa[f, to, HEAD_SIZE:] = marks[part]

    def sort_queries(p):
        rows = jnp.dot(turns[p], qbuf[p], preferred_element_type=F32).astype(BF16)
        for f in range(2):
            part = slice(f * SLOT, (f + 1) * SLOT)
            for g in range(GROUP):
                to = pl.ds(p * TILE + g * SLOT, SLOT)
                qa[f, to, 0:HEAD_SIZE] = rows[part, g * HEAD_SIZE : (g + 1) * HEAD_SIZE]

    BLOCK = 2048
    row_id = lax.broadcasted_iota(jnp.int32, (BLOCK, HALF), 0)
    col_id = lax.broadcasted_iota(jnp.int32, (BLOCK, HALF), 1)
    late_pos = (col_id & (SLOT - 1)) > (row_id & (SLOT - 1))

    def score(r, f, is_own):
        def block(n, carry):
            at = pl.ds(pl.multiple_of(n * BLOCK, BLOCK), BLOCK)
            s = lax.dot_general(qa[f, at, :], ks[f, r], NT, preferred_element_type=F32) * FACTOR
            if is_own:
                late = late_pos & ((col_id >> 5) == (row_id >> 8) + n * (BLOCK // TILE))
                s = jnp.where(late, NEG, s)
            sbuf[f, at, pl.ds(pl.multiple_of(r * HALF, HALF), HALF)] = s
            top = jnp.maximum(s[:, 0:128], s[:, 128:])
            mx[f, at, :] = top if is_own else jnp.maximum(mx[f, at, :], top)
            return carry

        lax.fori_loop(0, QROWS // BLOCK, block, 0)

    def sort_if(r):
        @pl.when(r <= z)
        def _():
            sort_keys(r)

        @pl.when((r > z) & (r < bound))
        def _():
            for f in range(2):
                ks[f, r, :, 0:HEAD_SIZE] = jnp.zeros((HALF, HEAD_SIZE), BF16)
                vs[f, pl.ds(pl.multiple_of(r * HALF, HALF), HALF), :] = jnp.zeros((HALF, HEAD_SIZE), BF16)

    def score_if(r):
        @pl.when(r < bound)
        def _():
            for f in range(2):
                score(r, f, False)

    def ready_queries():
        own[2].wait()
        for c in q_row:
            c.wait_recv()
        for p in range(N_HEAD):
            sort_queries(p)

    bound = jnp.where(z < N_SEQ // 2, N_SEQ // 2, N_SEQ)
    near = {(way, t): source(way, t) for way in range(2) for t in range(1, 4)}
    opposite = lax.rem(z + 4, N_SEQ)
    def mark_if(r):
        @pl.when(r < bound)
        def _():
            mark_keys(r)

    forward(1, 2)
    mark_keys(z)
    forward(1, 3)
    mark_if(near[0, 1])
    forward(2, 0)
    mark_if(near[1, 1])
    forward(2, 1)
    mark_if(near[0, 2])
    forward(2, 2)
    mark_if(near[1, 2])
    forward(2, 3)
    mark_if(near[0, 3])
    for p in range(N_HEAD // 2):
        mark_queries(p)
    forward(3, 0)
    mark_if(near[1, 3])
    for p in range(N_HEAD // 2, N_HEAD):
        mark_queries(p)
    forward(3, 1)
    mark_if(opposite)
    sort_keys(z)
    forward(3, 2)
    sort_if(near[0, 1])
    sort_if(near[1, 1])
    forward(3, 3)
    sort_if(near[0, 2])
    sort_if(near[1, 2])
    ready_queries()
    score(z, 0, True)
    score(z, 1, True)
    for way in range(2):
        score_if(near[way, 1])
        score_if(near[way, 2])
    forward(4, 0)
    forward(4, 2)
    for way in range(2):
        sort_if(near[way, 3])
        score_if(near[way, 3])
    forward(4, 1)
    forward(4, 3)
    sort_if(opposite)
    score_if(opposite)

    def tile(limit, step, carry):
        m = lax.rem(step, 3)
        across = jnp.where(step < 6, 2 - m + 3 * (m // 2), 0)
        other = jnp.where(step < 6, step // 3, 7 - step)
        p = lax.rem(h // 2 + across, 4) * 2 + lax.rem(h + other, 2)
        d = lax.rem(p - h + N_HEAD, N_HEAD)
        at = pl.ds(pl.multiple_of(p * TILE, TILE), TILE)
        keys = limit * HALF
        for f in range(2):
            top = jnp.broadcast_to(jnp.max(mx[f, at, :], axis=1, keepdims=True), (TILE, 128))
            weights = jnp.exp2(sbuf[f, at, 0:keys] - jnp.concatenate([top] * (keys // 128), axis=1))
            total = weights[:, 0:128]
            for n in range(1, keys // 128):
                total = total + weights[:, n * 128 : (n + 1) * 128]
            blend = jnp.dot(weights.astype(BF16), vs[f, 0:keys, :], preferred_element_type=F32)
            done = (blend / jnp.sum(total, axis=1, keepdims=True)).astype(BF16)
            for g in range(GROUP):
                osort[f * SLOT : (f + 1) * SLOT, g * HEAD_SIZE : (g + 1) * HEAD_SIZE] = done[
                    g * SLOT : (g + 1) * SLOT
                ]
        t = r1 - first_row(z, p)
        t = jnp.where(t < 0.0, t + TOK_W, t)
        back = jnp.where(c1 == t, 1.0, 0.0).astype(BF16)
        stage[p] = jnp.dot(back, osort[...], preferred_element_type=F32).astype(BF16)

        @pl.when(p != h)
        def _():
            remote(stage.at[p], out_ref.at[:, wide(h)], o_s.at[d], o_r.at[d], head=p).start()

        return carry

    for limit in (N_SEQ // 2, N_SEQ):

        @pl.when(bound == limit)
        def _():
            lax.fori_loop(0, N_HEAD, functools.partial(tile, limit), 0)

    last = pltpu.make_async_copy(stage.at[h], out_ref.at[:, wide(h)], own_sem.at[0])
    last.start()
    last.wait()
    for c in id_row + k_row + v_row + q_row + id_col + an_col:
        c.wait_send()
    for (way, t, j), c in ring.items():

        @pl.when(goes(way, t))
        def _():
            c.wait_send()

    for d in range(1, N_HEAD):
        p = lax.rem(h + d, N_HEAD)
        remote(stage.at[p], out_ref.at[:, wide(h)], o_s.at[d], o_r.at[d], head=p).wait()


def body(queries, keys, values, counts, offsets, tree_ids, block_lists):
    any_space = pl.BlockSpec(memory_space=pl.ANY)
    smem = pl.BlockSpec(memory_space=pltpu.SMEM)
    dma = pltpu.SemaphoreType.DMA
    return pl.pallas_call(
        kernel,
        out_shape=jax.ShapeDtypeStruct((TOK_W, KEY_VALUE_HEADS * WIDE), BF16),
        in_specs=[smem] * 4 + [pl.BlockSpec(memory_space=pltpu.HBM)] * 3,
        out_specs=any_space,
        scratch_shapes=[
            pltpu.VMEM((N_HEAD, TOK_W, WIDE), BF16),
            pltpu.VMEM((N_SEQ * ROW, 2 * HEAD_SIZE), BF16),
            pltpu.VMEM((2, N_SEQ, HALF, 2 * HEAD_SIZE), BF16),
            pltpu.VMEM((2, N_SEQ * HALF, HEAD_SIZE), BF16),
            pltpu.VMEM((N_SEQ, 2, FOUR, FOUR), BF16),
            pltpu.VMEM((N_HEAD, TOK_W, TOK_W), BF16),
            pltpu.VMEM((N_SEQ, N_HEAD, 1, 128), F32),
            pltpu.VMEM((N_SEQ, QB, 1, 128), F32),
            pltpu.VMEM((2, QROWS, 2 * HEAD_SIZE), BF16),
            pltpu.VMEM((2, QROWS, N_SEQ * HALF), F32),
            pltpu.VMEM((2, QROWS, 128), F32),
            pltpu.VMEM((TOK_W, WIDE), BF16),
            pltpu.VMEM((N_HEAD, TOK_W, WIDE), BF16),
            dma((3,)),
            dma((N_HEAD, 2)),
            dma((N_HEAD, 2)),
            dma((N_HEAD,)),
            dma((N_HEAD,)),
            dma((N_HEAD,)),
            dma((N_HEAD,)),
            dma((2, 4, 4)),
            dma((2, 4, 4)),
            dma((N_SEQ,)),
            dma((N_SEQ,)),
            dma((N_SEQ,)),
            dma((N_SEQ,)),
            dma((N_HEAD + 1,)),
            dma((N_HEAD + 1,)),
        ],
        compiler_params=pltpu.CompilerParams(
            collective_id=0, has_side_effects=True, vmem_limit_bytes=58 * 1024 * 1024
        ),
    )(counts, offsets, tree_ids, jnp.transpose(block_lists, (2, 0, 1)), queries, keys, values)


def solution(mesh):
    split = P(("rep", "seq", "head"), None)
    placed = (split,) * 6 + (P(("rep", "seq"), None, None),)
    return jax.shard_map(body, mesh=mesh, in_specs=placed, out_specs=split, check_vma=False)
```
